256 devices in a mesh: var: 32 (over z_lo, x, core), tok: 8 (over y, z_hi).
Axes of the slice: x: 4, y: 4, z: 8 (z_hi: 2, z_lo: 4; z = z_hi * 4 + z_lo), core: 2. Of those that a mesh axis runs over, the one named last changes fastest.
Arguments:
- patches: bfloat16 [64, 64, 4096], P('var', None, 'tok'), may hold values from -6 to 6
- embed_weight: bfloat16 [64, 64, 1024], P('var'), may hold values from -0.75 to 0.75
- var_embed: float32 [64, 1024], P('var'), may hold values from -3 to 3
- agg_keys: bfloat16 [16, 1024], replicated, may hold values from -1.796875 to 1.796875
- agg_value: bfloat16 [1024, 1024], replicated, may hold values from -0.1875 to 0.1875
- agg_out: bfloat16 [1024, 1024], replicated, may hold values from -0.1875 to 0.1875
- pos_embed: bfloat16 [4096, 1024], P(('tok', 'var')), may hold values from -3 to 3
- norm_first: float32 [1024], replicated, may hold values from 0.5 to 1.5
- norm_second: float32 [1024], replicated, may hold values from 0.5 to 1.5
- w_qkv: bfloat16 [3, 1024, 1024], P(None, None, 'tok'), may hold values from -0.25 to 0.25
- w_out: bfloat16 [1024, 1024], P('tok'), may hold values from -0.1875 to 0.1875
- w_up: bfloat16 [1024, 4096], P(None, 'tok'), may hold values from -0.1875 to 0.1875
- w_down: bfloat16 [4096, 1024], P('tok'), may hold values from -0.09375 to 0.09375
- cotangent: bfloat16 [4096, 1024], P(('tok', 'var')), may hold values from -6 to 6
Outputs:
- block_out: bfloat16 [4096, 1024], P(('tok', 'var'))
- grad_embed: float32 [64, 64, 1024], P('var', None, 'tok')
- grad_var_embed: float32 [64, 1024], P('var', 'tok')
The draws below stay inside these ranges and needn't reach their ends.
All inputs are finite; a program needn't handle non-finite values.
Results may differ from the reference program's by a relative error of at most 0.04.
Values may be sent and summed in bfloat16 or wider, within the bound.
A program may use at most 128 MiB of HBM per device.

```python
import jax
import jax.numpy as jnp
from jax import lax

D = 1024
HEADS = 16
HEAD_SIZE = 64
FF = 4096
VARS = 64
PIXELS = 64
SEQ = 4096


def levels(rng, dims, pieces, low, largest):
    def one(dim, shards_of):
        steps = jax.random.uniform(jax.random.fold_in(jax.random.fold_in(rng, 6), dim), (shards_of,), jnp.float32, low / len(pieces), largest / len(pieces))
        return jnp.repeat(jnp.exp(steps), dims[dim] // shards_of).reshape((-1,) + (1,) * (len(dims) - dim - 1))

    loudness = one(*pieces[0])
    for cut in pieces[1:]:
        loudness = loudness * one(*cut)
    return loudness


def bell_draw(rng, dims, scale, reach, cuts=(), kind=jnp.bfloat16):
    drawn = scale * jax.random.normal(rng, dims, jnp.float32)
    if cuts:
        drawn = drawn * levels(rng, dims, cuts, -0.22, 0.18)
    return jnp.clip(drawn, -reach, reach).astype(kind)


def setup_inputs(seed: int = 0) -> dict:
    arg_keys = jax.random.split(jax.random.key(seed), 15)
    return {
        "patches": bell_draw(arg_keys[0], (VARS, PIXELS, SEQ), 1.0, 6.0, ((0, 32), (2, 8))),
        "embed_weight": bell_draw(arg_keys[1], (VARS, PIXELS, D), PIXELS ** -0.5, 0.75, ((0, 32),)),
        "var_embed": bell_draw(arg_keys[2], (VARS, D), 0.5, 3.0, ((0, 32),), jnp.float32),
        "agg_keys": bell_draw(arg_keys[3], (HEADS, D), 0.3, 1.796875),
        "agg_value": bell_draw(arg_keys[4], (D, D), D ** -0.5, 0.1875),
        "agg_out": bell_draw(arg_keys[5], (D, D), D ** -0.5, 0.1875),
        "pos_embed": bell_draw(arg_keys[6], (SEQ, D), 0.5, 3.0, ((0, 256),)),
        "norm_first": jnp.clip(1.0 + 0.1 * jax.random.normal(arg_keys[7], (D,), jnp.float32), 0.5, 1.5),
        "norm_second": jnp.clip(1.0 + 0.1 * jax.random.normal(arg_keys[8], (D,), jnp.float32), 0.5, 1.5),
        "w_qkv": bell_draw(arg_keys[9], (3, D, D), (D // 2) ** -0.5, 0.25, ((2, 8),)),
        "w_out": bell_draw(arg_keys[10], (D, D), D ** -0.5, 0.1875, ((0, 8),)),
        "w_up": bell_draw(arg_keys[11], (D, FF), D ** -0.5, 0.1875, ((1, 8),)),
        "w_down": bell_draw(arg_keys[12], (FF, D), FF ** -0.5, 0.09375, ((0, 8),)),
        "cotangent": bell_draw(arg_keys[13], (SEQ, D), 1.0, 6.0, ((0, 256),)),
    }


EPS = 1e-05

def layer_norm(values, gain):
    mean = lax.optimization_barrier(jnp.mean(values, axis=-1, keepdims=True))
    centred = values - mean
    spread = lax.optimization_barrier(jnp.mean(centred * centred, axis=-1, keepdims=True))
    return centred * lax.rsqrt(spread + EPS) * gain

def smooth_gelu(values):
    return jax.nn.gelu(values, approximate=True)

def embed_block(patch_block, embed_weight, var_embed):
    product = jnp.einsum('vpn,vpd->vnd', patch_block.astype(jnp.float32), embed_weight.astype(jnp.float32))
    return (product + var_embed[:, None, :]).astype(jnp.bfloat16)

def pool_forward(embedded, agg_keys, agg_value, agg_out):
    heads, width = agg_keys.shape
    size = width // heads
    scale = size ** (-0.5)
    emb_wide = embedded.astype(jnp.float32)
    scores = jnp.einsum('vnd,hd->nhv', emb_wide, agg_keys.astype(jnp.float32)) * scale
    expo = jnp.exp(scores)
    probs = expo / lax.optimization_barrier(jnp.sum(expo, axis=-1, keepdims=True))
    probs_b = probs.astype(jnp.bfloat16)
    pooled = jnp.einsum('nhv,vnd->nhd', probs_b.astype(jnp.float32), emb_wide).astype(jnp.bfloat16)
    value_three = agg_value.reshape(width, heads, size).astype(jnp.float32)
    picked = jnp.einsum('nhd,dhe->nhe', pooled.astype(jnp.float32), value_three).astype(jnp.bfloat16)
    mixed = jnp.dot(picked.reshape(-1, width), agg_out, preferred_element_type=jnp.float32)
    return (mixed, (probs, probs_b))

def pool_backward(embedded, agg_keys, agg_value, agg_out, saved, grad_mixed):
    probs, probs_b = saved
    heads, width = agg_keys.shape
    size = width // heads
    scale = size ** (-0.5)
    grad_picked = jnp.dot(grad_mixed, agg_out.T, preferred_element_type=jnp.float32).astype(jnp.bfloat16)
    grad_picked = grad_picked.reshape(-1, heads, size)
    value_three = agg_value.reshape(width, heads, size).astype(jnp.float32)
    grad_pooled = jnp.einsum('nhe,dhe->nhd', grad_picked.astype(jnp.float32), value_three).astype(jnp.bfloat16)
    pooled_wide = grad_pooled.astype(jnp.float32)
    grad_pool = jnp.einsum('nhd,vnd->nhv', pooled_wide, embedded.astype(jnp.float32))
    inner = lax.optimization_barrier(jnp.sum(probs * grad_pool, axis=-1, keepdims=True))
    grad_pool_scores = (probs * (grad_pool - inner) * scale).astype(jnp.bfloat16)
    first = jnp.einsum('nhv,nhd->vnd', probs_b.astype(jnp.float32), pooled_wide)
    second = jnp.einsum('nhv,hd->vnd', grad_pool_scores.astype(jnp.float32), agg_keys.astype(jnp.float32))
    return (first + second).astype(jnp.bfloat16)

def reference(patches, embed_weight, var_embed, agg_keys, agg_value, agg_out, pos_embed, norm_first, norm_second, w_qkv, w_out, w_up, w_down, cotangent):
    width = D
    size = HEAD_SIZE
    scale = size ** (-0.5)
    token_block = min(SEQ, 512)
    token_count = SEQ // token_block
    query_block = min(SEQ, 256)
    query_count = SEQ // query_block

    def token_forward(index):
        patch_block = lax.dynamic_slice_in_dim(patches, index * token_block, token_block, 2)
        embedded = embed_block(patch_block, embed_weight, var_embed)
        return pool_forward(embedded, agg_keys, agg_value, agg_out)[0]
    mixed = lax.map(token_forward, jnp.arange(token_count, dtype=jnp.int32)).reshape(SEQ, width)
    x_first = mixed + pos_embed.astype(jnp.float32)
    normed_first = layer_norm(x_first, norm_first).astype(jnp.bfloat16)
    qkv = jnp.einsum('nd,sdc->nsc', normed_first.astype(jnp.float32), w_qkv.astype(jnp.float32)).astype(jnp.bfloat16)
    query = qkv[:, 0].reshape(SEQ, HEADS, size).astype(jnp.float32)
    keys = qkv[:, 1].reshape(SEQ, HEADS, size).astype(jnp.float32)
    values = qkv[:, 2].reshape(SEQ, HEADS, size).astype(jnp.float32)

    def attend(index):
        query_part = lax.dynamic_slice_in_dim(query, index * query_block, query_block, 0)
        scores = jnp.einsum('bhe,khe->hbk', query_part, keys) * scale
        expo = jnp.exp(scores)
        total = lax.optimization_barrier(jnp.sum(expo, axis=-1))
        numer = jnp.einsum('hbk,khe->bhe', expo.astype(jnp.bfloat16).astype(jnp.float32), values)
        return (numer / total.T[:, :, None], total.T)
    att, totals = lax.map(attend, jnp.arange(query_count, dtype=jnp.int32))
    att = att.reshape(SEQ, HEADS, size)
    totals = totals.reshape(SEQ, HEADS)
    att_b = att.astype(jnp.bfloat16).reshape(SEQ, width)
    x_second = x_first + jnp.dot(att_b, w_out, preferred_element_type=jnp.float32)
    normed_second = layer_norm(x_second, norm_second).astype(jnp.bfloat16)
    hidden_pre = jnp.dot(normed_second, w_up, preferred_element_type=jnp.float32)
    hidden = smooth_gelu(hidden_pre).astype(jnp.bfloat16)
    out_sum = x_second + jnp.dot(hidden, w_down, preferred_element_type=jnp.float32)
    block_out = out_sum.astype(jnp.bfloat16)
    grad_hidden = jnp.dot(cotangent, w_down.T, preferred_element_type=jnp.float32)
    _, gelu_back = jax.vjp(smooth_gelu, hidden_pre)
    grad_pre = gelu_back(grad_hidden)[0].astype(jnp.bfloat16)
    grad_normed_second = jnp.dot(grad_pre, w_up.T, preferred_element_type=jnp.float32)
    _, second_back = jax.vjp(lambda inner: layer_norm(inner, norm_second), x_second)
    grad_second = cotangent.astype(jnp.float32) + second_back(grad_normed_second)[0]
    grad_att = jnp.dot(grad_second.astype(jnp.bfloat16), w_out.T, preferred_element_type=jnp.float32).astype(jnp.bfloat16)
    grad_att = grad_att.reshape(SEQ, HEADS, size).astype(jnp.float32)
    delta = lax.optimization_barrier(jnp.sum(grad_att * att, axis=-1))

    def attend_back(carry, index):
        grad_keys, grad_values = carry
        start = index * query_block
        query_part = lax.dynamic_slice_in_dim(query, start, query_block, 0)
        grad_part = lax.dynamic_slice_in_dim(grad_att, start, query_block, 0)
        total_part = lax.dynamic_slice_in_dim(totals, start, query_block, 0)
        delta_part = lax.dynamic_slice_in_dim(delta, start, query_block, 0)
        scores = jnp.einsum('bhe,khe->hbk', query_part, keys) * scale
        probs = jnp.exp(scores) / total_part.T[:, :, None]
        probs_b = probs.astype(jnp.bfloat16).astype(jnp.float32)
        grad_probs = jnp.einsum('bhe,khe->hbk', grad_part, values)
        grad_scores = (probs * (grad_probs - delta_part.T[:, :, None]) * scale).astype(jnp.bfloat16).astype(jnp.float32)
        grad_query = jnp.einsum('hbk,khe->bhe', grad_scores, keys)
        grad_keys = grad_keys + jnp.einsum('hbk,bhe->khe', grad_scores, query_part)
        grad_values = grad_values + jnp.einsum('hbk,bhe->khe', probs_b, grad_part)
        return ((grad_keys, grad_values), grad_query)
    empty = jnp.zeros((SEQ, HEADS, size), jnp.float32)
    (grad_keys, grad_values), grad_query = lax.scan(attend_back, (empty, empty), jnp.arange(query_count, dtype=jnp.int32))
    grad_qkv = jnp.stack([grad_query.reshape(SEQ, width), grad_keys.reshape(SEQ, width), grad_values.reshape(SEQ, width)], axis=1).astype(jnp.bfloat16)
    grad_normed_first = jnp.einsum('nsc,sdc->nd', grad_qkv.astype(jnp.float32), w_qkv.astype(jnp.float32))
    _, first_back = jax.vjp(lambda inner: layer_norm(inner, norm_first), x_first)
    grad_first = grad_second + first_back(grad_normed_first)[0]
    grad_first_b = grad_first.astype(jnp.bfloat16)

    def token_back(carry, index):
        acc_embed, acc_var = carry
        patch_block = lax.dynamic_slice_in_dim(patches, index * token_block, token_block, 2)
        embedded = embed_block(patch_block, embed_weight, var_embed)
        _, saved = pool_forward(embedded, agg_keys, agg_value, agg_out)
        grad_block = lax.dynamic_slice_in_dim(grad_first_b, index * token_block, token_block, 0)
        grad_embedded = pool_backward(embedded, agg_keys, agg_value, agg_out, saved, grad_block).astype(jnp.float32)
        acc_embed = acc_embed + jnp.einsum('vpn,vnd->vpd', patch_block.astype(jnp.float32), grad_embedded)
        acc_var = acc_var + lax.optimization_barrier(jnp.sum(grad_embedded, axis=1))
        return ((acc_embed, acc_var), None)
    start_embed = jnp.zeros((VARS, PIXELS, width), jnp.float32)
    start_var = jnp.zeros((VARS, width), jnp.float32)
    (grad_embed, grad_var_embed), _ = lax.scan(token_back, (start_embed, start_var), jnp.arange(token_count, dtype=jnp.int32))
    return (block_out, grad_embed, grad_var_embed)
```

```python
import jax
import jax.numpy as jnp
from jax import lax
from jax.sharding import PartitionSpec as P

EPS = 1e-05


def layer_norm(values, gain):
    mean = jnp.mean(values, axis=-1, keepdims=True)
    centred = values - mean
    spread = jnp.mean(centred * centred, axis=-1, keepdims=True)
    return centred * lax.rsqrt(spread + EPS) * gain


def smooth_gelu(values):
    return jax.nn.gelu(values, approximate=True)


def score_block(query, key_block, value_block, grad_att, total, delta, scale):
    scores = (
        jnp.einsum("rhe,khe->hrk", query, key_block, preferred_element_type=jnp.float32) * scale
    )
    probs = jnp.exp(scores) / total[:, :, None]
    grad_probs = jnp.einsum(
        "rhe,khe->hrk", grad_att, value_block, preferred_element_type=jnp.float32
    )
    grad_scores = (probs * (grad_probs - delta.T[:, :, None]) * scale).astype(jnp.bfloat16)
    return (probs.astype(jnp.bfloat16), grad_scores)


def local(
    patches,
    embed_weight,
    var_embed,
    agg_keys,
    agg_value,
    agg_out,
    pos_embed,
    norm_first,
    norm_second,
    w_qkv,
    w_out,
    w_up,
    w_down,
    cotangent,
):
    var_count = lax.axis_size("var")
    var_local, pixels, span = patches.shape
    width = embed_weight.shape[2]
    rows = span // var_count
    heads = agg_keys.shape[0]
    size = width // heads
    scale = size ** (-0.5)
    local_width = w_out.shape[0]
    local_heads = local_width // size
    keyed = jnp.einsum("vpd,hd->vhp", embed_weight, agg_keys, preferred_element_type=jnp.float32)
    var_b = var_embed.astype(jnp.bfloat16)
    keyed_bias = jnp.einsum("vd,hd->vh", var_embed, agg_keys.astype(jnp.float32), precision="highest")
    scores = jnp.einsum(
        "vhp,vpn->vhn",
        keyed.astype(jnp.bfloat16),
        patches,
        preferred_element_type=jnp.float32,
    )
    expo_pool = jnp.exp((scores + keyed_bias[:, :, None]) * scale)
    pool_total = lax.psum(jnp.sum(expo_pool, axis=0), "var")
    probs = expo_pool / pool_total
    probs_b = probs.astype(jnp.bfloat16)
    valued = jnp.einsum(
        "vpd,dc->vpc", embed_weight, agg_value, preferred_element_type=jnp.float32
    ).astype(jnp.bfloat16)
    valued_bias = jnp.einsum("vd,dc->vc", var_b, agg_value, preferred_element_type=jnp.float32)
    valued_tokens = (
        jnp.einsum("vpn,vpc->vnc", patches, valued, preferred_element_type=jnp.float32)
        + valued_bias[:, None, :]
    )
    wide = jnp.repeat(jnp.swapaxes(probs_b, 1, 2), size, axis=2).astype(jnp.float32)
    picked = lax.psum_scatter(
        jnp.sum(wide * valued_tokens, axis=0).astype(jnp.bfloat16),
        "var",
        scatter_dimension=0,
        tiled=True,
    )
    mixed = jnp.dot(picked, agg_out, preferred_element_type=jnp.float32)
    x_first = mixed + pos_embed.astype(jnp.float32)
    normed_first = layer_norm(x_first, norm_first).astype(jnp.bfloat16)
    qkv = jnp.einsum(
        "nd,sdc->nsc",
        lax.all_gather(normed_first, "tok", axis=0, tiled=True),
        w_qkv,
        preferred_element_type=jnp.float32,
    ).astype(jnp.bfloat16)
    group = qkv.shape[0]
    query = qkv[:, 0].reshape(group, local_heads, size)
    keys_values = lax.all_gather(qkv[:, 1:], "var", axis=0, tiled=True)
    seq = keys_values.shape[0]
    block = 2048
    count = seq // block
    steps = jnp.arange(count, dtype=jnp.int32)

    def key_piece(index):
        piece = lax.dynamic_slice_in_dim(keys_values, index * block, block, 0)
        return (
            piece[:, 0].reshape(block, local_heads, size),
            piece[:, 1].reshape(block, local_heads, size),
        )

    def forward_step(carry, index):
        numer, total = carry
        key_block, value_block = key_piece(index)
        scores = (
            jnp.einsum("rhe,khe->hrk", query, key_block, preferred_element_type=jnp.float32) * scale
        )
        expo = jnp.exp(scores)
        total = total + jnp.sum(expo, axis=-1)
        numer = numer + jnp.einsum(
            "hrk,khe->rhe",
            expo.astype(jnp.bfloat16),
            value_block,
            preferred_element_type=jnp.float32,
        )
        return ((numer, total), None)

    start_numer = jnp.zeros((group, local_heads, size), jnp.float32)
    start_total = jnp.zeros((local_heads, group), jnp.float32)
    (numer, total), _ = lax.scan(forward_step, (start_numer, start_total), steps)
    att = numer / total.T[:, :, None]
    att_b = att.astype(jnp.bfloat16).reshape(group, local_width)
    x_second = x_first + lax.psum_scatter(
        jnp.dot(att_b, w_out, preferred_element_type=jnp.float32).astype(jnp.bfloat16),
        "tok",
        scatter_dimension=0,
        tiled=True,
    ).astype(jnp.float32)
    normed_second = layer_norm(x_second, norm_second).astype(jnp.bfloat16)
    hidden_pre = jnp.dot(
        lax.all_gather(normed_second, "tok", axis=0, tiled=True),
        w_up,
        preferred_element_type=jnp.float32,
    )
    hidden = smooth_gelu(hidden_pre).astype(jnp.bfloat16)
    out_sum = x_second + lax.psum_scatter(
        jnp.dot(hidden, w_down, preferred_element_type=jnp.float32).astype(jnp.bfloat16),
        "tok",
        scatter_dimension=0,
        tiled=True,
    ).astype(jnp.float32)
    block_out = out_sum.astype(jnp.bfloat16)
    grad_hidden = jnp.einsum(
        "nd,fd->nf",
        lax.all_gather(cotangent, "tok", axis=0, tiled=True),
        w_down,
        preferred_element_type=jnp.float32,
    )
    _, gelu_back = jax.vjp(smooth_gelu, hidden_pre)
    grad_pre = gelu_back(grad_hidden)[0].astype(jnp.bfloat16)
    part = grad_pre
    grad_normed_second = lax.psum_scatter(
        jnp.einsum("nf,df->nd", part, w_up, preferred_element_type=jnp.float32).astype(
            jnp.bfloat16
        ),
        "tok",
        scatter_dimension=0,
        tiled=True,
    ).astype(jnp.float32)
    _, second_back = jax.vjp(lambda inner: layer_norm(inner, norm_second), x_second)
    grad_second = cotangent.astype(jnp.float32) + second_back(grad_normed_second)[0]
    grad_att_flat = jnp.einsum(
        "nd,cd->nc",
        lax.all_gather(grad_second.astype(jnp.bfloat16), "tok", axis=0, tiled=True),
        w_out,
        preferred_element_type=jnp.float32,
    ).astype(jnp.bfloat16)
    grad_att = grad_att_flat.reshape(group, local_heads, size)
    delta = jnp.sum(grad_att.astype(jnp.float32) * att, axis=-1)

    def backward_step(grad_query, index):
        key_block, value_block = key_piece(index)
        probs_b, grad_scores = score_block(
            query, key_block, value_block, grad_att, total, delta, scale
        )
        grad_query = grad_query + jnp.einsum(
            "hrk,khe->rhe", grad_scores, key_block, preferred_element_type=jnp.float32
        )
        grad_key = jnp.einsum(
            "hrk,rhe->khe", grad_scores, query, preferred_element_type=jnp.float32
        )
        grad_value = jnp.einsum(
            "hrk,rhe->khe", probs_b, grad_att, preferred_element_type=jnp.float32
        )
        return (
            grad_query,
            jnp.stack(
                [grad_key.reshape(block, local_width), grad_value.reshape(block, local_width)],
                axis=1,
            ),
        )

    grad_query, key_terms = lax.scan(backward_step, start_numer, steps)
    own_kv = lax.psum_scatter(
        key_terms.reshape(seq, 2, local_width).astype(jnp.bfloat16),
        "var",
        scatter_dimension=0,
        tiled=True,
    ).astype(jnp.float32)
    grad_qkv = jnp.concatenate([grad_query.reshape(group, 1, local_width), own_kv], axis=1).astype(
        jnp.bfloat16
    )
    part = grad_qkv
    grad_normed_first = lax.psum_scatter(
        jnp.einsum("nsc,sdc->nd", part, w_qkv, preferred_element_type=jnp.float32).astype(
            jnp.bfloat16
        ),
        "tok",
        scatter_dimension=0,
        tiled=True,
    ).astype(jnp.float32)
    _, first_back = jax.vjp(lambda inner: layer_norm(inner, norm_first), x_first)
    grad_first = grad_second + first_back(grad_normed_first)[0]
    grad_picked = jnp.einsum(
        "nk,dk->nd",
        grad_first.astype(jnp.bfloat16),
        agg_out,
        preferred_element_type=jnp.float32,
    ).astype(jnp.bfloat16)
    grad_picked_all = lax.all_gather(grad_picked, "var", axis=0, tiled=True)
    picked_all = lax.all_gather(picked, "var", axis=0, tiled=True)
    gp = grad_picked_all.astype(jnp.float32)
    inner = jnp.sum((gp * picked_all.astype(jnp.float32)).reshape(span, heads, size), axis=2).T
    grad_pool = jnp.swapaxes(
        jnp.sum((gp[None] * valued_tokens).reshape(var_local, span, heads, size), axis=3), 1, 2
    )
    grad_pool_scores = (probs * (grad_pool - inner[None]) * scale).astype(jnp.bfloat16)
    weighted = (wide * gp[None]).astype(jnp.bfloat16)
    value_term = jnp.einsum(
        "vpn,vnc->vpc", patches, weighted, preferred_element_type=jnp.float32
    ).astype(jnp.bfloat16)
    key_term = jnp.einsum(
        "vpn,vhn->vph", patches, grad_pool_scores, preferred_element_type=jnp.float32
    ).astype(jnp.bfloat16)
    embed_term = jnp.einsum(
        "vpc,dc->vpd", value_term, agg_value, preferred_element_type=jnp.float32
    ) + jnp.einsum("vph,hd->vpd", key_term, agg_keys, preferred_element_type=jnp.float32)
    var_term = jnp.einsum(
        "vc,dc->vd",
        jnp.sum(weighted, axis=1, dtype=jnp.float32).astype(jnp.bfloat16),
        agg_value,
        preferred_element_type=jnp.float32,
    ) + jnp.einsum(
        "vh,hd->vd",
        jnp.sum(grad_pool_scores, axis=2, dtype=jnp.float32).astype(jnp.bfloat16),
        agg_keys,
        preferred_element_type=jnp.float32,
    )
    grad_embed, grad_var_embed = (
        lax.psum_scatter(
            embed_term.astype(jnp.bfloat16), "tok", scatter_dimension=2, tiled=True
        ).astype(jnp.float32),
        lax.psum_scatter(
            var_term.astype(jnp.bfloat16), "tok", scatter_dimension=1, tiled=True
        ).astype(jnp.float32),
    )
    return (block_out, grad_embed, grad_var_embed)


def solution(mesh):
    in_specs = (
        P("var", None, "tok"),
        P("var", None, None),
        P("var", None),
        P(),
        P(),
        P(),
        P(("tok", "var"), None),
        P(),
        P(),
        P(None, None, "tok"),
        P("tok", None),
        P(None, "tok"),
        P("tok", None),
        P(("tok", "var"), None),
    )
    out_specs = (P(("tok", "var"), None), P("var", None, "tok"), P("var", "tok"))
    return jax.shard_map(local, mesh=mesh, in_specs=in_specs, out_specs=out_specs, check_vma=False)
```

```python
import jax
import jax.numpy as jnp
from jax import lax
from jax.experimental import pallas as pl
from jax.experimental.pallas import tpu as pltpu
from jax.sharding import PartitionSpec as P

EPS = 1e-05
MESH = pl.DeviceIdType.MESH
BF = jnp.bfloat16
F32 = jnp.float32

NZ, NX, NC, NY, NH = 4, 4, 2, 4, 2
ROWS, WIDTH, HEADS, SIZE, PIX = 16, 1024, 16, 64, 64
SPAN = 512
EXT = 80
GWIDTH = WIDTH + 128
LINKS = 160
SCALE = SIZE ** (-0.5)


def mm(a, b):
    return lax.dot_general(a, b, (((1,), (0,)), ((), ())), preferred_element_type=F32)


def mm_nt(a, b):
    return lax.dot_general(a, b, (((1,), (1,)), ((), ())), preferred_element_type=F32)


def norm_parts(values):
    mean = jnp.mean(values, axis=-1, keepdims=True)
    centred = values - mean
    spread = jnp.mean(centred * centred, axis=-1, keepdims=True)
    rstd = lax.rsqrt(spread + EPS)
    return centred * rstd, rstd


def norm_back(grad, hat, rstd, gain):
    inner = grad * gain
    first = jnp.mean(inner, axis=-1, keepdims=True)
    second = jnp.mean(inner * hat, axis=-1, keepdims=True)
    return rstd * (inner - first - hat * second)


def gelu_both(values):
    c = 0.7978845608028654
    a = 0.044715
    square = values * values
    t = jnp.tanh(c * values * (1.0 + a * square))
    half = 0.5 * (1.0 + t)
    slope = half + 0.5 * values * (1.0 - t * t) * c * (1.0 + 3.0 * a * square)
    return values * half, slope


SCRATCH = dict(
    px=((2, EXT, SPAN), BF),
    wx=((128, WIDTH), BF),
    akey=((16, WIDTH), BF),
    vemb=((2, WIDTH), F32),
    aval=((WIDTH, WIDTH), BF),
    aout=((WIDTH, WIDTH), BF),
    posv=((ROWS, WIDTH), BF),
    g1=((1, WIDTH), F32),
    g2=((1, WIDTH), F32),
    wq=((WIDTH, 384), BF),
    wo=((128, WIDTH), BF),
    wu=((WIDTH, 512), BF),
    wd=((512, WIDTH), BF),
    tsend=((2, 16, SPAN), BF),
    trecv=((10, 16, SPAN), BF),
    town=((16, SPAN), F32),
    expo=((32, SPAN), F32),
    ub=((2, 128, WIDTH), BF),
    ubias=((16, WIDTH), F32),
    ptl=((NZ, NX, 32, 128), BF),
    prl=((NZ, NX, 32, 128), F32),
    spread=((2, 128, WIDTH), BF),
    vals=((2, NZ, NX, 32, WIDTH), BF),
    part=((NZ, NX, NC, ROWS, WIDTH), BF),
    rc1=((NX, NZ, ROWS, WIDTH), BF),
    s1=((NX - 1, NZ, ROWS, WIDTH), BF),
    rm1=((2, NZ // 2, ROWS, WIDTH), BF),
    rx1=((2, NZ, ROWS, WIDTH), BF),
    own1=((NZ, ROWS, WIDTH), F32),
    s2=((NZ - 1, ROWS, WIDTH), BF),
    rz1=((NZ - 1, ROWS, WIDTH), BF),
    picked=((ROWS, WIDTH), F32),
    xh1=((ROWS, WIDTH), F32),
    xh2=((NH, ROWS, WIDTH), F32),
    xa=((NH, ROWS, WIDTH), F32),
    xb=((NH, ROWS, WIDTH), F32),
    gsec=((NH, ROWS, WIDTH), F32),
    xnear=((ROWS, WIDTH), BF),
    xfar=((ROWS, WIDTH), BF),
    bsz=((2, NH, ROWS, WIDTH), BF),
    brz=((2, NH, ROWS, WIDTH), BF),
    nf1=((NY, NH, ROWS, WIDTH), BF),
    cot=((NY, NH, ROWS, WIDTH), BF),
    nf2=((NY, NH, ROWS, WIDTH), BF),
    gsa=((NY, NH, ROWS, WIDTH), BF),
    tsrc=((4, NY, NH, ROWS, WIDTH), BF),
    try_=((4, NY - 1, NH, ROWS, WIDTH), BF),
    tsz=((4, ROWS, WIDTH), BF),
    trz=((4, ROWS, WIDTH), BF),
    fsrc=((NY, NH, 2 * EXT, 128), BF),
    fry=((NY - 1, NH, 2 * EXT, 128), BF),
    fsz=((2 * EXT, 128), BF),
    frz=((2 * EXT, 128), BF),
    qs=((256, 128), BF),
    kvb=((NZ, NX, NC, 128, 256), BF),
    es=((NX, NZ, 256, 256), BF),
    numt=((128, 256), F32),
    tot=((8, 256), F32),
    inv=((128, 128), F32),
    att=((128, 128), F32),
    gb=((256, 128), BF),
    dp=((NZ, NX, NC, 128, 256), BF),
    rc2=((NX, NZ, 128, 256), BF),
    s1b=((NX - 1, NZ, 128, 256), BF),
    rm2=((2, NZ // 2, 128, 256), BF),
    rx2=((2, NZ, 128, 256), BF),
    own2=((NZ, 128, 256), F32),
    s2b=((NZ - 1, 128, 256), BF),
    rz2=((NZ - 1, 128, 256), BF),
    gpre=((128, 512), BF),
    hid=((128, 512), BF),
    gpb=((NZ, NX, NC, ROWS, GWIDTH), BF),
    zs=((2, NZ, NX, 32, WIDTH), BF),
    gps=((NZ, NX, 32, 128), BF),
    kext=((128, WIDTH), BF),
)


ARGS = (
    "patches",
    "embed",
    "var_e",
    "keys",
    "a_val",
    "a_out",
    "pos",
    "n1",
    "n2",
    "wqkv",
    "w_out",
    "w_up",
    "w_down",
    "cotangent",
)
OUTS = ("out_ref", "sum_ref")


class Refs:
    pass


def kernel(*refs):
    names = ARGS + OUTS + tuple(SCRATCH)
    s = Refs()
    for name, ref in zip(names, refs):
        setattr(s, name, ref)
    send_sems, recv_sems, load_sems = refs[len(names) :]

    v = lax.axis_index("var")
    t = lax.axis_index("tok")
    c = lax.rem(v, 2)
    x = lax.rem(lax.div(v, 2), 4)
    z = lax.div(v, 8)
    y = lax.div(t, 2)
    h = lax.rem(t, 2)

    def turn(i, k):
        return lax.rem(i + k, 4)

    def dev(zz=None, xx=None, cc=None, yy=None, hh=None):
        zz = z if zz is None else zz
        xx = x if xx is None else xx
        cc = c if cc is None else cc
        yy = y if yy is None else yy
        hh = h if hh is None else hh
        return ((zz * 4 + xx) * 2 + cc, yy * 2 + hh)

    sibling = dev(cc=1 - c)
    partner = dev(hh=1 - h)
    started = []

    def send(src, dst, device):
        index = len(started)
        copy = pltpu.make_async_remote_copy(
            src_ref=src,
            dst_ref=dst,
            send_sem=send_sems.at[index],
            recv_sem=recv_sems.at[index],
            device_id=device,
            device_id_type=MESH,
        )
        copy.start()
        started.append(copy)
        return copy

    loads = []

    def load(src, dst):
        copy = pltpu.make_async_copy(src, dst, load_sems.at[len(loads)])
        copy.start()
        loads.append(copy)
        return copy

    l_first = [
        load(s.keys, s.akey),
        load(s.embed, s.wx),
        load(s.patches.at[0], s.px.at[0, pl.ds(0, PIX)]),
        load(s.patches.at[1], s.px.at[1, pl.ds(0, PIX)]),
        load(s.var_e, s.vemb),
    ]
    l_val = load(s.a_val, s.aval)
    l_cot = load(s.cotangent, s.cot.at[y, h])
    l_mix = [load(s.a_out, s.aout), load(s.pos, s.posv), load(s.n1, s.g1)]
    l_qkv = [load(s.wqkv.at[i], s.wq.at[:, pl.ds(i * 128, 128)]) for i in range(3)]
    l_wo = load(s.w_out, s.wo)
    l_mlp = [load(s.n2, s.g2), load(s.w_up, s.wu), load(s.w_down, s.wd)]

    peers = [sibling, partner]
    for k in (1, 2, 3):
        peers += [dev(zz=turn(z, k)), dev(xx=turn(x, k)), dev(yy=turn(y, k))]
        peers += [dev(xx=turn(x, k), cc=1 - c)]
    barrier = pltpu.get_barrier_semaphore()
    for peer in peers:
        pl.semaphore_signal(barrier, inc=1, device_id=peer, device_id_type=MESH)

    lane_head = lax.broadcasted_iota(jnp.int32, (128, WIDTH), 1) // SIZE
    row = lax.broadcasted_iota(jnp.int32, (128, WIDTH), 0)
    for i in range(2):
        s.spread[i] = jnp.where(row == lane_head + i * 16, 1.0, 0.0).astype(BF)
        ones = lax.broadcasted_iota(jnp.int32, (EXT - PIX, SPAN), 0)
        s.px[i, PIX:EXT] = jnp.where(ones == 0, 1.0, 0.0).astype(BF)

    for copy in l_first:
        copy.wait()
    key_t = mm_nt(s.akey[...], s.wx[...])
    both = jnp.concatenate([key_t, key_t], axis=0)
    rows32 = lax.broadcasted_iota(jnp.int32, (32, 128), 0) // 16
    lanes32 = lax.broadcasted_iota(jnp.int32, (32, 128), 1) // PIX
    both = jnp.where(rows32 == lanes32, both, 0.0).astype(BF)
    rows16 = lax.broadcasted_iota(jnp.int32, (16, WIDTH), 0)
    var_rows = jnp.where(
        rows16 == 0, s.vemb[0:1, :], jnp.where(rows16 == 1, s.vemb[1:2, :], 0.0)
    ).astype(BF)
    key_bias = mm_nt(s.akey[...], var_rows)
    bias32 = jnp.concatenate([key_bias[:, 0:1], key_bias[:, 1:2]], axis=0)
    pixels = jnp.concatenate([s.px[0, 0:PIX], s.px[1, 0:PIX]], axis=0)
    expo = jnp.exp((mm(both, pixels) + bias32) * SCALE)
    s.expo[...] = expo
    s.town[...] = expo[0:16] + expo[16:32]
    s.tsend[0] = s.town[...].astype(BF)
    s.ptl[...] = jnp.transpose(pixels).reshape(NZ, NX, 32, 128)

    pl.semaphore_wait(barrier, len(peers))
    t_near = [send(s.tsend.at[0], s.trecv.at[0], sibling)]
    for k in (2, 1, 3):
        t_near.append(send(s.tsend.at[0], s.trecv.at[2 * k - 1], dev(xx=turn(x, k))))
        t_near.append(send(s.tsend.at[0], s.trecv.at[2 * k], dev(xx=turn(x, k), cc=1 - c)))

    def gather_tok_start(buf):
        first = send(buf.at[y, h], buf.at[y, h], partner)
        direct = [
            send(buf.at[y, h], buf.at[y, h], dev(yy=turn(y, k))) for k in (2, 1, 3)
        ]
        return buf, first, direct

    def gather_tok_end(state):
        buf, first, direct = state
        first.wait_recv()
        passed = [
            send(buf.at[y, 1 - h], buf.at[y, 1 - h], dev(yy=turn(y, k))) for k in (2, 1, 3)
        ]
        for copy in direct + passed:
            copy.wait_recv()

    l_cot.wait()
    l_val.wait()
    bias = mm(var_rows, s.aval[...])
    s.ubias[...] = bias
    row_var = lax.broadcasted_iota(jnp.int32, (128, 256), 0) // PIX
    for n in range(4):
        cols = pl.ds(n * 256, 256)
        u = mm(s.wx[...], s.aval[:, cols])
        for i in range(2):
            s.ub[i, :, cols] = jnp.where(row_var == i, u, 0.0).astype(BF)

    def value_step(i, carry):
        lhs = s.ptl[i].reshape(128, 128)
        for j in range(2):
            out = mm(lhs, s.ub[j]) + s.ubias[j : j + 1, :]
            s.vals[j, i] = out.astype(BF).reshape(NX, 32, WIDTH)
        return carry

    lax.fori_loop(0, 2, value_step, 0)
    for copy in t_near:
        copy.wait_recv()
    near = s.town[...]
    for i in range(7):
        near = near + s.trecv[i].astype(F32)
    s.town[...] = near
    s.tsend[1] = near.astype(BF)
    t_z = [send(s.tsend.at[1], s.trecv.at[6 + k], dev(zz=turn(z, k))) for k in (2, 1, 3)]
    lax.fori_loop(2, 4, value_step, 0)
    for copy in t_z:
        copy.wait_recv()
    total = s.town[...]
    for i in range(7, 10):
        total = total + s.trecv[i].astype(F32)
    probs = s.expo[...] / jnp.concatenate([total, total], axis=0)
    probs = jnp.concatenate([probs, jnp.zeros((96, SPAN), F32)], axis=0)
    s.prl[...] = jnp.transpose(probs).reshape(NZ, NX, 32, 128)

    def sum_var(produce, part, rc, s1, rm, rx, own, s2, rz):
        core, middle, over_x = {}, {}, []
        right, left = dev(xx=turn(x, 1)), dev(xx=turn(x, 3))
        low, high = pl.ds(0, NZ // 2), pl.ds(NZ // 2, NZ // 2)

        def finish(k):
            core[k].wait_recv()
            xk = turn(x, k)
            total = part[:, xk, c].astype(F32) + rc[k].astype(F32)
            if k == 0:
                own[...] = total
                return
            s1[k - 1] = total.astype(BF)
            if k == 2:
                middle[1] = send(s1.at[1, low], rm.at[0], right)
                middle[3] = send(s1.at[1, high], rm.at[1], left)
            if k == 1:
                over_x.append(send(s1.at[0, high], rx.at[0, high], right))
            if k == 3:
                over_x.append(send(s1.at[2, low], rx.at[1, low], left))

        def relay(k):
            middle[k].wait_recv()
            if k == 1:
                s1[0, low] = (s1[0, low].astype(F32) + rm[0].astype(F32)).astype(BF)
                over_x.append(send(s1.at[0, low], rx.at[0, low], right))
            else:
                s1[2, high] = (s1[2, high].astype(F32) + rm[1].astype(F32)).astype(BF)
                over_x.append(send(s1.at[2, high], rx.at[1, high], left))

        previous = None
        for k in (2, 1, 3, 0):
            xk = turn(x, k)
            produce(xk)
            core[k] = send(part.at[:, xk, 1 - c], rc.at[k], sibling)
            if previous is not None:
                finish(previous)
            if previous == 3:
                relay(1)
                relay(3)
            previous = k
        finish(previous)
        for copy in over_x:
            copy.wait_recv()

        def here(zk):
            return own[zk] + rx[0, zk].astype(F32) + rx[1, zk].astype(F32)

        over_z = []
        for k in (2, 1, 3):
            zk = turn(z, k)
            s2[k - 1] = here(zk).astype(BF)
            over_z.append(send(s2.at[k - 1], rz.at[k - 1], dev(zz=zk)))
        mine = here(z)
        for copy in over_z:
            copy.wait_recv()
        return mine + rz[0].astype(F32) + rz[1].astype(F32) + rz[2].astype(F32)

    def pool_produce(xk):
        probs_b = s.prl[:, xk].reshape(128, 128).astype(BF)
        acc = None
        for j in range(2):
            term = mm(probs_b, s.spread[j]) * s.vals[j, :, xk].reshape(128, WIDTH).astype(F32)
            acc = term if acc is None else acc + term
        s.part[:, xk] = acc.astype(BF).reshape(NZ, NC, ROWS, WIDTH)

    cot_state = gather_tok_start(s.cot)
    picked = sum_var(pool_produce, s.part, s.rc1, s.s1, s.rm1, s.rx1, s.own1, s.s2, s.rz1)
    picked_b = picked.astype(BF)
    s.picked[...] = picked_b.astype(F32)

    for copy in l_mix:
        copy.wait()
    x_first = mm(picked_b, s.aout[...]) + s.posv[...].astype(F32)
    s.xa[h] = x_first
    s.xnear[...] = x_first.astype(BF)
    hat, rstd1 = norm_parts(x_first)
    s.xh1[...] = hat
    s.nf1[y, h] = (hat * s.g1[...]).astype(BF)
    state = gather_tok_start(s.nf1)
    gather_tok_end(cot_state)
    x_copy = send(s.xnear, s.xfar, partner)
    gather_tok_end(state)
    for copy in l_qkv:
        copy.wait()
    qkv = mm(s.nf1[...].reshape(128, WIDTH), s.wq[...])
    s.kvb[z, x, c] = qkv[:, 128:384].astype(BF)

    def gather_var_start(buf):
        mine = buf.at[z, x, c]
        right, left = dev(xx=turn(x, 1)), dev(xx=turn(x, 3))
        over_z = [send(mine, mine, dev(zz=turn(z, k))) for k in (1, 2, 3)]
        over_x = {(0, 1): send(mine, mine, right), (0, 3): send(mine, mine, left)}
        over_c = {(0, 0): send(mine, mine, sibling)}
        return buf, over_z, over_x, over_c

    def gather_var_pass(state):
        buf, over_z, over_x, over_c = state
        right, left = dev(xx=turn(x, 1)), dev(xx=turn(x, 3))
        for kz in (1, 3, 2):
            over_z[kz - 1].wait_recv()
            block = buf.at[turn(z, 4 - kz), x, c]
            over_x[kz, 1] = send(block, block, right)
            over_x[kz, 3] = send(block, block, left)
            over_c[kz, 0] = send(block, block, sibling)

    def gather_var_end(state):
        buf, over_z, over_x, over_c = state
        right, left = dev(xx=turn(x, 1)), dev(xx=turn(x, 3))
        for kz in (0, 1, 3, 2):
            for kx in (1, 3):
                over_x[kz, kx].wait_recv()
                block = buf.at[turn(z, 4 - kz), turn(x, 4 - kx), c]
                if kx == 1 and kz in (0, 1):
                    over_x[kz, 2] = send(block, block, right)
                if kx == 3 and kz in (2, 3):
                    over_x[kz, 2] = send(block, block, left)
                over_c[kz, kx] = send(block, block, sibling)

    def gather_var_far(state):
        buf, over_z, over_x, over_c = state
        for kz in (0, 1, 3, 2):
            over_x[kz, 2].wait_recv()
            block = buf.at[turn(z, 4 - kz), turn(x, 2), c]
            over_c[kz, 2] = send(block, block, sibling)

    def gather_var_core(state, kx):
        for kz in range(4):
            state[3][kz, kx].wait_recv()

    kv_state = gather_var_start(s.kvb)
    lane128 = lax.broadcasted_iota(jnp.int32, (128, 128), 1)
    row128 = lax.broadcasted_iota(jnp.int32, (128, 128), 0)

    def by_head(values):
        zero = jnp.zeros_like(values)
        return jnp.concatenate(
            [jnp.where(lane128 < SIZE, values, zero), jnp.where(lane128 >= SIZE, values, zero)],
            axis=0,
        ).astype(BF)

    def own_head(values):
        return jnp.where(row128 < SIZE, values[:, 0:128], values[:, 128:256])

    query = qkv[:, 0:128].astype(BF).astype(F32) * SCALE
    s.qs[...] = by_head(query)
    s.numt[...] = jnp.zeros((128, 256), F32)
    s.tot[...] = jnp.zeros((8, 256), F32)
    gather_var_pass(kv_state)

    def attend(xk):
        def step(i, carry):
            block = s.kvb[pl.ds(i * 2, 2), xk].reshape(512, 256)
            scores = mm_nt(block[:, 0:128], s.qs[...])
            e = jnp.exp(scores)
            e_b = e.astype(BF)
            s.es[xk, pl.ds(i * 2, 2)] = e_b.reshape(2, 256, 256)
            s.tot[...] += jnp.sum(e.reshape(64, 8, 256), axis=0)
            s.numt[...] += mm(jnp.transpose(block[:, 128:256].astype(F32)).astype(BF), e_b)
            return carry

        lax.fori_loop(0, 2, step, 0)

    gather_var_core(kv_state, 0)
    attend(x)
    gather_var_end(kv_state)
    gather_var_core(kv_state, 1)
    attend(turn(x, 3))
    gather_var_far(kv_state)
    gather_var_core(kv_state, 3)
    attend(turn(x, 1))
    gather_var_core(kv_state, 2)
    attend(turn(x, 2))

    inverse = 1.0 / jnp.sum(s.tot[...], axis=0, keepdims=True)
    inv_t = own_head(jnp.broadcast_to(inverse, (128, 256)))
    s.inv[...] = jnp.transpose(inv_t)
    att = jnp.transpose(own_head(s.numt[...]) * inv_t)
    s.att[...] = att

    def sum_tok_start(i, values):
        s.tsrc[i] = values.astype(BF).reshape(NY, NH, ROWS, WIDTH)
        return [
            send(s.tsrc.at[i, turn(y, k)], s.try_.at[i, k - 1], dev(yy=turn(y, k)))
            for k in (2, 1, 3)
        ]

    def sum_tok_pass(i, over_y):
        for copy in over_y:
            copy.wait_recv()

        def here(hh):
            return (
                s.tsrc[i, y, hh].astype(F32)
                + s.try_[i, 0, hh].astype(F32)
                + s.try_[i, 1, hh].astype(F32)
                + s.try_[i, 2, hh].astype(F32)
            )

        s.tsz[i] = here(1 - h).astype(BF)
        copy = send(s.tsz.at[i], s.trz.at[i], partner)
        return copy, here(h)

    def sum_tok_end(i, state):
        copy, mine = state
        copy.wait_recv()
        return mine + s.trz[i].astype(F32)

    def sum_tok_both(i, over_y):
        for copy in over_y:
            copy.wait_recv()
        mine = s.tsrc[i, y].astype(F32)
        for k in range(3):
            mine = mine + s.try_[i, k].astype(F32)
        s.bsz[i] = mine.astype(BF)
        copy = send(s.bsz.at[i], s.brz.at[i], partner)
        copy.wait_recv()
        return (mine + s.brz[i].astype(F32)).reshape(2 * ROWS, WIDTH)

    def gather_y_start(buf):
        return [send(buf.at[y], buf.at[y], dev(yy=turn(y, k))) for k in (2, 1, 3)]

    def both_rows(ref):
        return ref[...].reshape(2 * ROWS, WIDTH)

    l_wo.wait()
    over_y = sum_tok_start(0, mm(att.astype(BF), s.wo[...]))
    for copy in l_mlp:
        copy.wait()
    grad_hidden = mm_nt(s.cot[...].reshape(128, WIDTH), s.wd[...])
    x_copy.wait_recv()
    s.xa[1 - h] = s.xfar[...].astype(F32)
    x_second = both_rows(s.xa) + sum_tok_both(0, over_y)
    s.xb[...] = x_second.reshape(NH, ROWS, WIDTH)
    hat2, rstd2 = norm_parts(x_second)
    s.xh2[...] = hat2.reshape(NH, ROWS, WIDTH)
    s.nf2[y] = (hat2 * s.g2[...]).astype(BF).reshape(NH, ROWS, WIDTH)
    for copy in gather_y_start(s.nf2):
        copy.wait_recv()
    hidden_pre = mm(s.nf2[...].reshape(128, WIDTH), s.wu[...])
    hidden, slope = gelu_both(hidden_pre)
    s.hid[...] = hidden.astype(BF)
    grad_pre = (slope * grad_hidden).astype(BF)
    over_y = sum_tok_start(1, mm_nt(grad_pre, s.wu[...]))
    out_y = sum_tok_start(2, mm(s.hid[...], s.wd[...]))
    grad_normed = sum_tok_both(1, over_y)
    both_cot = s.cot[y].astype(F32).reshape(2 * ROWS, WIDTH)
    grad_second = both_cot + norm_back(grad_normed, both_rows(s.xh2), rstd2, s.g2[...])
    s.gsec[...] = grad_second.reshape(NH, ROWS, WIDTH)
    s.gsa[y] = grad_second.astype(BF).reshape(NH, ROWS, WIDTH)
    over_y = gather_y_start(s.gsa)
    out_state = sum_tok_pass(2, out_y)
    for copy in over_y:
        copy.wait_recv()

    grad_att = mm_nt(s.gsa[...].reshape(128, WIDTH), s.wo[...]).astype(BF)
    grad_over = (grad_att.astype(F32) * s.inv[...]).astype(BF)
    s.gb[...] = by_head(grad_over.astype(F32))
    product = jnp.transpose(grad_over.astype(F32) * s.att[...])
    delta = jnp.concatenate(
        [
            jnp.sum(product[0:SIZE], axis=0, keepdims=True),
            jnp.sum(product[SIZE:128], axis=0, keepdims=True),
        ],
        axis=1,
    )
    s.tot[0:1, :] = delta
    s.numt[...] = jnp.zeros((128, 256), F32)

    def attend_back(xk):
        def step(i, carry):
            block = s.kvb[pl.ds(i * 2, 2), xk].reshape(512, 256)
            e_b = s.es[xk, pl.ds(i * 2, 2)].reshape(512, 256)
            ahead = mm_nt(block[:, 128:256], s.gb[...])
            d_b = (e_b.astype(F32) * (ahead - s.tot[0:1, :])).astype(BF)
            s.numt[...] += mm(jnp.transpose(block[:, 0:128].astype(F32)).astype(BF), d_b)
            grad_key = mm(d_b, s.qs[...]).astype(BF)
            grad_value = mm(e_b, s.gb[...]).astype(BF)
            s.dp[pl.ds(i * 2, 2), xk] = jnp.concatenate([grad_key, grad_value], axis=1).reshape(
                2, NC, 128, 256
            )
            return carry

        lax.fori_loop(0, 2, step, 0)

    own_kv = sum_var(attend_back, s.dp, s.rc2, s.s1b, s.rm2, s.rx2, s.own2, s.s2b, s.rz2)
    grad_query = jnp.transpose(own_head(s.numt[...])) * SCALE
    grad_qkv = jnp.concatenate([grad_query.astype(BF), own_kv.astype(BF)], axis=1)
    over_y = sum_tok_start(3, mm_nt(grad_qkv, s.wq[...]))
    s.out_ref[...] = (s.xb[h] + sum_tok_end(2, out_state)).astype(BF)
    grad_normed = sum_tok_end(3, sum_tok_pass(3, over_y))
    grad_first = s.gsec[h] + norm_back(grad_normed, s.xh1[...], rstd1, s.g1[...])

    grad_picked = mm_nt(grad_first.astype(BF), s.aout[...]).astype(BF)
    inner = mm_nt((grad_picked.astype(F32) * s.picked[...]).astype(BF), s.spread[0] + s.spread[1])
    s.gpb[z, x, c] = jnp.concatenate([grad_picked, inner.astype(BF)], axis=1)
    gp_state = gather_var_start(s.gpb)
    rows_k = lax.broadcasted_iota(jnp.int32, (128, WIDTH), 0)
    keys8 = jnp.concatenate([s.akey[...]] * 8, axis=0)
    s.kext[...] = jnp.where(rows_k < 32, keys8.astype(F32), 0.0).astype(BF)
    gather_var_pass(gp_state)

    def pool_back(xk):
        block = s.gpb[:, xk].reshape(128, GWIDTH)
        grad = block[:, 0:WIDTH].astype(F32)
        probs = s.prl[:, xk].reshape(128, 128)
        probs_b = probs.astype(BF)
        ahead = None
        for j in range(2):
            term = (grad * s.vals[j, :, xk].reshape(128, WIDTH).astype(F32)).astype(BF)
            term = mm_nt(term, s.spread[j])
            ahead = term if ahead is None else ahead + term
            wide = mm(probs_b, s.spread[j])
            s.zs[j, :, xk] = (wide * grad).astype(BF).reshape(NZ, 32, WIDTH)
        scores = probs * (ahead - block[:, WIDTH:GWIDTH].astype(F32)) * SCALE
        s.gps[:, xk] = scores.astype(BF).reshape(NZ, 32, 128)

    gather_var_core(gp_state, 0)
    pool_back(x)
    gather_var_end(gp_state)
    gather_var_core(gp_state, 1)
    pool_back(turn(x, 3))
    gather_var_far(gp_state)
    gather_var_core(gp_state, 3)
    pool_back(turn(x, 1))
    gather_var_core(gp_state, 2)
    pool_back(turn(x, 2))

    key_part = mm(s.px[...].reshape(2 * EXT, SPAN), s.gps[...].reshape(SPAN, 128))
    rows160 = lax.broadcasted_iota(jnp.int32, (2 * EXT, 128), 0) // EXT
    lanes160 = lax.broadcasted_iota(jnp.int32, (2 * EXT, 128), 1) // 16
    key_part = jnp.where(rows160 == lanes160, key_part, 0.0).astype(BF)
    value_part = jnp.concatenate(
        [mm(s.px[j], s.zs[j].reshape(SPAN, WIDTH)).astype(BF) for j in range(2)], axis=0
    )
    for n in range(4):
        cols = pl.ds(n * 256, 256)
        term = mm_nt(value_part, s.aval[cols, :]) + mm(key_part, s.kext[:, cols])
        term = term.astype(BF)
        for i in range(2):
            s.fsrc[n, i] = term[:, i * 128 : (i + 1) * 128]
    last = [
        send(s.fsrc.at[turn(y, k)], s.fry.at[k - 1], dev(yy=turn(y, k))) for k in (2, 1, 3)
    ]
    for copy in last:
        copy.wait_recv()

    def here(hh):
        return (
            s.fsrc[y, hh].astype(F32)
            + s.fry[0, hh].astype(F32)
            + s.fry[1, hh].astype(F32)
            + s.fry[2, hh].astype(F32)
        )

    s.fsz[...] = here(1 - h).astype(BF)
    copy = send(s.fsz, s.frz, partner)
    mine = here(h)
    copy.wait_recv()
    final = mine + s.frz[...].astype(F32)
    s.sum_ref[...] = final
    for copy in started:
        copy.wait_send()


def finish_kernel(out_ref, sum_ref, block_ref, embed_ref, var_ref):
    block_ref[...] = out_ref[...]
    for j in range(2):
        embed_ref[j] = sum_ref[j * EXT : j * EXT + PIX]
        var_ref[j : j + 1, :] = sum_ref[j * EXT + PIX : j * EXT + PIX + 1]


def local(
    patches,
    embed_weight,
    var_embed,
    agg_keys,
    agg_value,
    agg_out,
    pos_embed,
    norm_first,
    norm_second,
    w_qkv,
    w_out,
    w_up,
    w_down,
    cotangent,
):
    anywhere = pl.BlockSpec(memory_space=pl.ANY)
    vmem = pl.BlockSpec(memory_space=pltpu.VMEM)
    results = pl.pallas_call(
        kernel,
        out_shape=(
            jax.ShapeDtypeStruct((ROWS, WIDTH), BF),
            jax.ShapeDtypeStruct((2 * EXT, 128), F32),
        ),
        in_specs=[anywhere] * 14,
        out_specs=(vmem, vmem),
        scratch_shapes=[pltpu.VMEM(shape, dtype) for shape, dtype in SCRATCH.values()]
        + [
            pltpu.SemaphoreType.DMA((LINKS,)),
            pltpu.SemaphoreType.DMA((LINKS,)),
            pltpu.SemaphoreType.DMA((20,)),
        ],
        compiler_params=pltpu.CompilerParams(
            collective_id=0, has_side_effects=True, vmem_limit_bytes=56 * 1024 * 1024
        ),
    )(
        patches,
        embed_weight.reshape(2 * PIX, WIDTH),
        var_embed,
        agg_keys,
        agg_value,
        agg_out,
        pos_embed,
        norm_first.reshape(1, WIDTH),
        norm_second.reshape(1, WIDTH),
        w_qkv,
        w_out,
        w_up,
        w_down,
        cotangent,
    )
    return pl.pallas_call(
        finish_kernel,
        out_shape=(
            jax.ShapeDtypeStruct((ROWS, WIDTH), BF),
            jax.ShapeDtypeStruct((2, PIX, 128), F32),
            jax.ShapeDtypeStruct((2, 128), F32),
        ),
        in_specs=[vmem, vmem],
        out_specs=(vmem, vmem, vmem),
    )(*results)


def solution(mesh):
    in_specs = (
        P("var", None, "tok"),
        P("var", None, None),
        P("var", None),
        P(),
        P(),
        P(),
        P(("tok", "var"), None),
        P(),
        P(),
        P(None, None, "tok"),
        P("tok", None),
        P(None, "tok"),
        P("tok", None),
        P(("tok", "var"), None),
    )
    out_specs = (P(("tok", "var"), None), P("var", None, "tok"), P("var", "tok"))
    return jax.shard_map(local, mesh=mesh, in_specs=in_specs, out_specs=out_specs, check_vma=False)
```

```python
import jax
import jax.numpy as jnp
from jax import lax
from jax.experimental import pallas as pl
from jax.experimental.pallas import tpu as pltpu
from jax.sharding import PartitionSpec as P

EPS = 1e-05
MESH = pl.DeviceIdType.MESH
BF = jnp.bfloat16
F32 = jnp.float32

NZ, NX, NC, NY, NH = 4, 4, 2, 4, 2
ROWS, WIDTH, HEADS, SIZE, PIX = 16, 1024, 16, 64, 64
SPAN = 512
EXT = 80
GWIDTH = WIDTH + 128
LINKS = 160
SCALE = SIZE ** (-0.5)


def mm(a, b):
    return lax.dot_general(a, b, (((1,), (0,)), ((), ())), preferred_element_type=F32)


def mm_nt(a, b):
    return lax.dot_general(a, b, (((1,), (1,)), ((), ())), preferred_element_type=F32)


def norm_parts(values):
    mean = jnp.mean(values, axis=-1, keepdims=True)
    centred = values - mean
    spread = jnp.mean(centred * centred, axis=-1, keepdims=True)
    rstd = lax.rsqrt(spread + EPS)
    return centred * rstd, rstd


def norm_back(grad, hat, rstd, gain):
    inner = grad * gain
    first = jnp.mean(inner, axis=-1, keepdims=True)
    second = jnp.mean(inner * hat, axis=-1, keepdims=True)
    return rstd * (inner - first - hat * second)


def gelu_both(values):
    c = 0.7978845608028654
    a = 0.044715
    square = values * values
    t = jnp.tanh(c * values * (1.0 + a * square))
    half = 0.5 * (1.0 + t)
    slope = half + 0.5 * values * (1.0 - t * t) * c * (1.0 + 3.0 * a * square)
    return values * half, slope


SCRATCH = dict(
    px=((2, EXT, SPAN), BF),
    wx=((128, WIDTH), BF),
    akey=((16, WIDTH), BF),
    vemb=((2, WIDTH), F32),
    aval=((WIDTH, WIDTH), BF),
    aout=((WIDTH, WIDTH), BF),
    posv=((ROWS, WIDTH), BF),
    g1=((1, WIDTH), F32),
    g2=((1, WIDTH), F32),
    wq=((WIDTH, 384), BF),
    wo=((128, WIDTH), BF),
    wu=((WIDTH, 512), BF),
    wd=((512, WIDTH), BF),
    tsend=((2, 16, SPAN), BF),
    trecv=((10, 16, SPAN), BF),
    town=((16, SPAN), F32),
    expo=((32, SPAN), F32),
    ub=((2, 128, WIDTH), BF),
    ubias=((16, WIDTH), F32),
    ptl=((NZ, NX, 32, 128), BF),
    prl=((NZ, NX, 32, 128), F32),
    spread=((2, 128, WIDTH), BF),
    vals=((2, NZ, NX, 32, WIDTH), BF),
    part=((NZ, NX, NC, ROWS, WIDTH), BF),
    rc1=((NX, NZ, ROWS, WIDTH), BF),
    s1=((NX - 1, NZ, ROWS, WIDTH), BF),
    rx1=((3, NZ, ROWS, WIDTH), BF),
    own1=((NZ, ROWS, WIDTH), F32),
    s2=((NZ - 1, ROWS, WIDTH), BF),
    rz1=((NZ - 1, ROWS, WIDTH), BF),
    picked=((ROWS, WIDTH), F32),
    xh1=((ROWS, WIDTH), F32),
    xh2=((NH, ROWS, WIDTH), F32),
    xa=((NH, ROWS, WIDTH), F32),
    xb=((NH, ROWS, WIDTH), F32),
    gsec=((NH, ROWS, WIDTH), F32),
    xnear=((ROWS, WIDTH), BF),
    xfar=((ROWS, WIDTH), BF),
    bsz=((2, NH, ROWS, WIDTH), BF),
    brz=((2, NH, ROWS, WIDTH), BF),
    nf1=((NY, NH, ROWS, WIDTH), BF),
    cot=((NY, NH, ROWS, WIDTH), BF),
    nf2=((NY, NH, ROWS, WIDTH), BF),
    gsa=((NY, NH, ROWS, WIDTH), BF),
    tsrc=((4, NY, NH, ROWS, WIDTH), BF),
    try_=((4, NY - 1, NH, ROWS, WIDTH), BF),
    tsz=((4, ROWS, WIDTH), BF),
    trz=((4, ROWS, WIDTH), BF),
    fsrc=((NY, NH, 2 * EXT, 128), BF),
    fry=((NY - 1, NH, 2 * EXT, 128), BF),
    fsz=((2 * EXT, 128), BF),
    frz=((2 * EXT, 128), BF),
    qs=((256, 128), BF),
    kvb=((NZ, NX, NC, 128, 256), BF),
    es=((NX, NZ, 256, 256), BF),
    numt=((128, 256), F32),
    tot=((8, 256), F32),
    inv=((128, 128), F32),
    att=((128, 128), F32),
    gb=((256, 128), BF),
    dpk=((NZ, NX, NC, 128, 128), BF),
    rck=((NX, NZ, 128, 128), BF),
    s1k=((NX - 1, NZ, 128, 128), BF),
    rmk=((2, NZ // 2, 128, 128), BF),
    rxk=((2, NZ, 128, 128), BF),
    ownk=((NZ, 128, 128), F32),
    s2k=((NZ - 1, 128, 128), BF),
    rzk=((NZ - 1, 128, 128), BF),
    dpv=((NZ, NX, NC, 128, 128), BF),
    rcv=((NX, NZ, 128, 128), BF),
    s1v=((NX - 1, NZ, 128, 128), BF),
    rmv=((2, NZ // 2, 128, 128), BF),
    rxv=((2, NZ, 128, 128), BF),
    ownv=((NZ, 128, 128), F32),
    s2v=((NZ - 1, 128, 128), BF),
    rzv=((NZ - 1, 128, 128), BF),
    hid=((128, 512), BF),
    gpb=((NZ, NX, NC, ROWS, GWIDTH), BF),
    zs=((2, NZ, NX, 32, WIDTH), BF),
    gps=((NZ, NX, 32, 128), BF),
    kext=((128, WIDTH), BF),
)


ARGS = (
    "patches",
    "embed",
    "var_e",
    "keys",
    "a_val",
    "a_out",
    "pos",
    "n1",
    "n2",
    "wqkv",
    "w_out",
    "w_up",
    "w_down",
    "cotangent",
)
OUTS = ("out_ref", "sum_ref")


class Refs:
    pass


def kernel(*refs):
    names = ARGS + OUTS + tuple(SCRATCH)
    s = Refs()
    for name, ref in zip(names, refs):
        setattr(s, name, ref)
    send_sems, recv_sems, load_sems = refs[len(names) :]

    v = lax.axis_index("var")
    t = lax.axis_index("tok")
    c = lax.rem(v, 2)
    x = lax.rem(lax.div(v, 2), 4)
    z = lax.div(v, 8)
    y = lax.div(t, 2)
    h = lax.rem(t, 2)

    def turn(i, k):
        return lax.rem(i + k, 4)

    def dev(zz=None, xx=None, cc=None, yy=None, hh=None):
        zz = z if zz is None else zz
        xx = x if xx is None else xx
        cc = c if cc is None else cc
        yy = y if yy is None else yy
        hh = h if hh is None else hh
        return ((zz * 4 + xx) * 2 + cc, yy * 2 + hh)

    sibling = dev(cc=1 - c)
    partner = dev(hh=1 - h)
    started = []

    def send(src, dst, device):
        index = len(started)
        copy = pltpu.make_async_remote_copy(
            src_ref=src,
            dst_ref=dst,
            send_sem=send_sems.at[index],
            recv_sem=recv_sems.at[index],
            device_id=device,
            device_id_type=MESH,
        )
        copy.start()
        started.append(copy)
        return copy

    settled = [0, 0]

    def settle():
        for copy in started[settled[0] : settled[1]]:
            copy.wait_send()
        settled[:] = settled[1], len(started)

    loads = []

    def load(src, dst):
        copy = pltpu.make_async_copy(src, dst, load_sems.at[len(loads)])
        copy.start()
        loads.append(copy)
        return copy

    l_first = [
        load(s.keys, s.akey),
        load(s.embed, s.wx),
        load(s.patches.at[0], s.px.at[0, pl.ds(0, PIX)]),
        load(s.patches.at[1], s.px.at[1, pl.ds(0, PIX)]),
        load(s.var_e, s.vemb),
    ]
    l_val = load(s.a_val, s.aval)
    l_cot = load(s.cotangent, s.cot.at[y, h])
    l_mix = [load(s.a_out, s.aout), load(s.pos, s.posv), load(s.n1, s.g1)]
    l_qkv = [load(s.wqkv.at[i], s.wq.at[:, pl.ds(i * 128, 128)]) for i in range(3)]
    l_wo = load(s.w_out, s.wo)
    l_mlp = [load(s.n2, s.g2), load(s.w_up, s.wu), load(s.w_down, s.wd)]

    peers = [sibling, partner]
    for k in (1, 2, 3):
        peers += [dev(zz=turn(z, k)), dev(xx=turn(x, k)), dev(yy=turn(y, k))]
        peers += [dev(xx=turn(x, k), cc=1 - c)]
    barrier = pltpu.get_barrier_semaphore()
    for peer in peers:
        pl.semaphore_signal(barrier, inc=1, device_id=peer, device_id_type=MESH)

    lane_head = lax.broadcasted_iota(jnp.int32, (128, WIDTH), 1) // SIZE
    row = lax.broadcasted_iota(jnp.int32, (128, WIDTH), 0)
    for i in range(2):
        s.spread[i] = jnp.where(row == lane_head + i * 16, 1.0, 0.0).astype(BF)
        ones = lax.broadcasted_iota(jnp.int32, (EXT - PIX, SPAN), 0)
        s.px[i, PIX:EXT] = jnp.where(ones == 0, 1.0, 0.0).astype(BF)

    for copy in l_first:
        copy.wait()
    key_t = mm_nt(s.akey[...], s.wx[...])
    both = jnp.concatenate([key_t, key_t], axis=0)
    rows32 = lax.broadcasted_iota(jnp.int32, (32, 128), 0) // 16
    lanes32 = lax.broadcasted_iota(jnp.int32, (32, 128), 1) // PIX
    both = jnp.where(rows32 == lanes32, both, 0.0).astype(BF)
    rows16 = lax.broadcasted_iota(jnp.int32, (16, WIDTH), 0)
    var_rows = jnp.where(
        rows16 == 0, s.vemb[0:1, :], jnp.where(rows16 == 1, s.vemb[1:2, :], 0.0)
    ).astype(BF)
    key_bias = mm_nt(s.akey[...], var_rows)
    bias32 = jnp.concatenate([key_bias[:, 0:1], key_bias[:, 1:2]], axis=0)
    pixels = jnp.concatenate([s.px[0, 0:PIX], s.px[1, 0:PIX]], axis=0)
    expo = jnp.exp((mm(both, pixels) + bias32) * SCALE)
    s.expo[...] = expo
    s.town[...] = expo[0:16] + expo[16:32]
    s.tsend[0] = s.town[...].astype(BF)
    s.ptl[...] = jnp.transpose(pixels).reshape(NZ, NX, 32, 128)

    pl.semaphore_wait(barrier, len(peers))
    t_near = [send(s.tsend.at[0], s.trecv.at[0], sibling)]
    for k in (2, 1, 3):
        t_near.append(send(s.tsend.at[0], s.trecv.at[2 * k - 1], dev(xx=turn(x, k))))
        t_near.append(send(s.tsend.at[0], s.trecv.at[2 * k], dev(xx=turn(x, k), cc=1 - c)))

    def gather_tok_start(buf):
        first = send(buf.at[y, h], buf.at[y, h], partner)
        direct = [
            send(buf.at[y, h], buf.at[y, h], dev(yy=turn(y, k))) for k in (2, 1, 3)
        ]
        return buf, first, direct

    def gather_tok_end(state):
        buf, first, direct = state
        first.wait_recv()
        settle()
        passed = [
            send(buf.at[y, 1 - h], buf.at[y, 1 - h], dev(yy=turn(y, k))) for k in (2, 1, 3)
        ]
        for copy in direct + passed:
            copy.wait_recv()

    l_cot.wait()
    l_val.wait()
    bias = mm(var_rows, s.aval[...])
    s.ubias[...] = bias
    row_var = lax.broadcasted_iota(jnp.int32, (128, 256), 0) // PIX
    for n in range(4):
        cols = pl.ds(n * 256, 256)
        u = mm(s.wx[...], s.aval[:, cols])
        for i in range(2):
            s.ub[i, :, cols] = jnp.where(row_var == i, u, 0.0).astype(BF)

    def value_step(i, carry):
        lhs = s.ptl[i].reshape(128, 128)
        for j in range(2):
            out = mm(lhs, s.ub[j]) + s.ubias[j : j + 1, :]
            s.vals[j, i] = out.astype(BF).reshape(NX, 32, WIDTH)
        return carry

    lax.fori_loop(0, 2, value_step, 0)
    for copy in t_near:
        copy.wait_recv()
    near = s.town[...]
    for i in range(7):
        near = near + s.trecv[i].astype(F32)
    s.town[...] = near
    s.tsend[1] = near.astype(BF)
    t_z = [send(s.tsend.at[1], s.trecv.at[6 + k], dev(zz=turn(z, k))) for k in (2, 1, 3)]
    lax.fori_loop(2, 4, value_step, 0)
    for copy in t_z:
        copy.wait_recv()
    total = s.town[...]
    for i in range(7, 10):
        total = total + s.trecv[i].astype(F32)
    probs = s.expo[...] / jnp.concatenate([total, total], axis=0)
    probs = jnp.concatenate([probs, jnp.zeros((96, SPAN), F32)], axis=0)
    s.prl[...] = jnp.transpose(probs).reshape(NZ, NX, 32, 128)

    class VarSum:
        def __init__(self, part, rc, s1, rm, rx, own, s2, rz):
            self.part, self.rc, self.s1, self.rm = part, rc, s1, rm
            self.rx, self.own, self.s2, self.rz = rx, own, s2, rz
            self.core, self.middle, self.over_x, self.over_z = {}, {}, [], []
            self.right, self.left = dev(xx=turn(x, 1)), dev(xx=turn(x, 3))
            self.low, self.high = pl.ds(0, NZ // 2), pl.ds(NZ // 2, NZ // 2)

        def put(self, k):
            self.core[k] = send(self.part.at[:, turn(x, k), 1 - c], self.rc.at[k], sibling)

        def pass_x(self, src, dst, device):
            self.over_x.append(send(src, dst, device))

        def finish(self, k):
            self.core[k].wait_recv()
            s1, rx, low, high = self.s1, self.rx, self.low, self.high
            total = self.part[:, turn(x, k), c].astype(F32) + self.rc[k].astype(F32)
            if k == 0:
                self.own[...] = total
                return
            s1[k - 1] = total.astype(BF)
            if self.rm is None:
                self.pass_x(s1.at[k - 1], rx.at[k - 1], dev(xx=turn(x, k)))
            elif k == 2:
                self.middle[1] = send(s1.at[1, low], self.rm.at[0], self.right)
                self.middle[3] = send(s1.at[1, high], self.rm.at[1], self.left)
            elif k == 1:
                self.pass_x(s1.at[0, high], rx.at[0, high], self.right)
            else:
                self.pass_x(s1.at[2, low], rx.at[1, low], self.left)

        def relay(self):
            if self.rm is None:
                return
            s1, rm, rx, low, high = self.s1, self.rm, self.rx, self.low, self.high
            self.middle[1].wait_recv()
            s1[0, low] = (s1[0, low].astype(F32) + rm[0].astype(F32)).astype(BF)
            self.pass_x(s1.at[0, low], rx.at[0, low], self.right)
            self.middle[3].wait_recv()
            s1[2, high] = (s1[2, high].astype(F32) + rm[1].astype(F32)).astype(BF)
            self.pass_x(s1.at[2, high], rx.at[1, high], self.left)

        def here(self, zk):
            total = self.own[zk]
            for i in range(self.rx.shape[0]):
                total = total + self.rx[i, zk].astype(F32)
            return total

        def along_z(self):
            for copy in self.over_x:
                copy.wait_recv()
            for k in (2, 1, 3):
                zk = turn(z, k)
                self.s2[k - 1] = self.here(zk).astype(BF)
                self.over_z.append(send(self.s2.at[k - 1], self.rz.at[k - 1], dev(zz=zk)))

        def end(self):
            mine = self.here(z)
            settle()
            for copy in self.over_z:
                copy.wait_recv()
            rz = self.rz
            return mine + rz[0].astype(F32) + rz[1].astype(F32) + rz[2].astype(F32)

    def pool_produce(xk):
        probs_b = s.prl[:, xk].reshape(128, 128).astype(BF)
        acc = None
        for j in range(2):
            term = mm(probs_b, s.spread[j]) * s.vals[j, :, xk].reshape(128, WIDTH).astype(F32)
            acc = term if acc is None else acc + term
        s.part[:, xk] = acc.astype(BF).reshape(NZ, NC, ROWS, WIDTH)

    cot_state = gather_tok_start(s.cot)
    pool_sum = VarSum(s.part, s.rc1, s.s1, None, s.rx1, s.own1, s.s2, s.rz1)
    for k, before in ((2, None), (1, 2), (3, 1), (0, 3)):
        pool_produce(turn(x, k))
        pool_sum.put(k)
        if before is not None:
            pool_sum.finish(before)
    pool_sum.finish(0)
    settle()
    pool_sum.along_z()
    picked = pool_sum.end()
    picked_b = picked.astype(BF)
    s.picked[...] = picked_b.astype(F32)

    for copy in l_mix:
        copy.wait()
    x_first = mm(picked_b, s.aout[...]) + s.posv[...].astype(F32)
    s.xa[h] = x_first
    s.xnear[...] = x_first.astype(BF)
    hat, rstd1 = norm_parts(x_first)
    s.xh1[...] = hat
    s.nf1[y, h] = (hat * s.g1[...]).astype(BF)
    state = gather_tok_start(s.nf1)
    gather_tok_end(cot_state)
    x_copy = send(s.xnear, s.xfar, partner)
    gather_tok_end(state)
    for copy in l_qkv:
        copy.wait()
    qkv = mm(s.nf1[...].reshape(128, WIDTH), s.wq[...])
    s.kvb[z, x, c] = qkv[:, 128:384].astype(BF)

    def gather_var_start(buf, direct):
        mine = buf.at[z, x, c]
        right, left = dev(xx=turn(x, 1)), dev(xx=turn(x, 3))
        over_z = [send(mine, mine, dev(zz=turn(z, k))) for k in (1, 2, 3)]
        over_x = {(0, 1): send(mine, mine, right), (0, 3): send(mine, mine, left)}
        if direct:
            over_x[0, 2] = send(mine, mine, dev(xx=turn(x, 2)))
        over_c = {(0, 0): send(mine, mine, sibling)}
        settle()
        return buf, over_z, over_x, over_c, direct

    def gather_var_pass(state):
        buf, over_z, over_x, over_c, direct = state
        right, left = dev(xx=turn(x, 1)), dev(xx=turn(x, 3))
        for kz in (1, 3, 2):
            over_z[kz - 1].wait_recv()
            block = buf.at[turn(z, 4 - kz), x, c]
            over_x[kz, 1] = send(block, block, right)
            over_x[kz, 3] = send(block, block, left)
            if direct:
                over_x[kz, 2] = send(block, block, dev(xx=turn(x, 2)))
            over_c[kz, 0] = send(block, block, sibling)

    def gather_var_end(state):
        buf, over_z, over_x, over_c, direct = state
        right, left = dev(xx=turn(x, 1)), dev(xx=turn(x, 3))
        for kz in (0, 1, 3, 2):
            for kx in (1, 3):
                over_x[kz, kx].wait_recv()
                block = buf.at[turn(z, 4 - kz), turn(x, 4 - kx), c]
                if kx == 1 and kz in (0, 1) and not direct:
                    over_x[kz, 2] = send(block, block, right)
                if kx == 3 and kz in (2, 3) and not direct:
                    over_x[kz, 2] = send(block, block, left)
                over_c[kz, kx] = send(block, block, sibling)

    def gather_var_far(state):
        buf, over_z, over_x, over_c, direct = state
        for kz in (0, 1, 3, 2):
            over_x[kz, 2].wait_recv()
            block = buf.at[turn(z, 4 - kz), turn(x, 2), c]
            over_c[kz, 2] = send(block, block, sibling)

    def gather_var_core(state, kx):
        for kz in range(4):
            state[3][kz, kx].wait_recv()

    kv_state = gather_var_start(s.kvb, False)
    lane128 = lax.broadcasted_iota(jnp.int32, (128, 128), 1)
    row128 = lax.broadcasted_iota(jnp.int32, (128, 128), 0)

    def by_head(values):
        zero = jnp.zeros_like(values)
        return jnp.concatenate(
            [jnp.where(lane128 < SIZE, values, zero), jnp.where(lane128 >= SIZE, values, zero)],
            axis=0,
        ).astype(BF)

    def own_head(values):
        return jnp.where(row128 < SIZE, values[:, 0:128], values[:, 128:256])

    query = qkv[:, 0:128].astype(BF).astype(F32) * SCALE
    s.qs[...] = by_head(query)
    s.numt[...] = jnp.zeros((128, 256), F32)
    s.tot[...] = jnp.zeros((8, 256), F32)
    gather_var_pass(kv_state)

    def attend(xk):
        def step(i):
            block = s.kvb[pl.ds(i * 2, 2), xk].reshape(512, 256)
            scores = mm_nt(block[:, 0:128], s.qs[...])
            e = jnp.exp(scores)
            e_b = e.astype(BF)
            s.es[xk, pl.ds(i * 2, 2)] = e_b.reshape(2, 256, 256)
            s.tot[...] += jnp.sum(e.reshape(64, 8, 256), axis=0)
            s.numt[...] += mm(jnp.transpose(block[:, 128:256].astype(F32)).astype(BF), e_b)

        for i in range(2):
            step(i)

    gather_var_end(kv_state)
    gather_var_core(kv_state, 0)
    attend(x)
    gather_var_core(kv_state, 1)
    attend(turn(x, 3))
    gather_var_far(kv_state)
    gather_var_core(kv_state, 3)
    attend(turn(x, 1))
    gather_var_core(kv_state, 2)
    attend(turn(x, 2))

    inverse = 1.0 / jnp.sum(s.tot[...], axis=0, keepdims=True)
    inv_t = own_head(jnp.broadcast_to(inverse, (128, 256)))
    s.inv[...] = jnp.transpose(inv_t)
    att = jnp.transpose(own_head(s.numt[...]) * inv_t)
    s.att[...] = att

    def sum_tok_start(i, values):
        s.tsrc[i] = values.astype(BF).reshape(NY, NH, ROWS, WIDTH)
        return [
            send(s.tsrc.at[i, turn(y, k)], s.try_.at[i, k - 1], dev(yy=turn(y, k)))
            for k in (2, 1, 3)
        ]

    def sum_tok_pass(i, over_y):
        for copy in over_y:
            copy.wait_recv()

        def here(hh):
            return (
                s.tsrc[i, y, hh].astype(F32)
                + s.try_[i, 0, hh].astype(F32)
                + s.try_[i, 1, hh].astype(F32)
                + s.try_[i, 2, hh].astype(F32)
            )

        s.tsz[i] = here(1 - h).astype(BF)
        copy = send(s.tsz.at[i], s.trz.at[i], partner)
        return copy, here(h)

    def sum_tok_end(i, state):
        copy, mine = state
        copy.wait_recv()
        return mine + s.trz[i].astype(F32)

    def sum_tok_both(i, over_y, beside=None):
        for copy in over_y:
            copy.wait_recv()
        mine = s.tsrc[i, y].astype(F32)
        for k in range(3):
            mine = mine + s.try_[i, k].astype(F32)
        s.bsz[i] = mine.astype(BF)
        copy = send(s.bsz.at[i], s.brz.at[i], partner)
        if beside is not None:
            beside()
        settle()
        copy.wait_recv()
        return (mine + s.brz[i].astype(F32)).reshape(2 * ROWS, WIDTH)

    def gather_y_start(buf):
        return [send(buf.at[y], buf.at[y], dev(yy=turn(y, k))) for k in (2, 1, 3)]

    def both_rows(ref):
        return ref[...].reshape(2 * ROWS, WIDTH)

    l_wo.wait()
    over_y = sum_tok_start(0, mm(att.astype(BF), s.wo[...]))
    for copy in l_mlp:
        copy.wait()
    grad_hidden = mm_nt(s.cot[...].reshape(128, WIDTH), s.wd[...])
    x_copy.wait_recv()
    s.xa[1 - h] = s.xfar[...].astype(F32)
    x_second = both_rows(s.xa) + sum_tok_both(0, over_y)
    s.xb[...] = x_second.reshape(NH, ROWS, WIDTH)
    hat2, rstd2 = norm_parts(x_second)
    s.xh2[...] = hat2.reshape(NH, ROWS, WIDTH)
    s.nf2[y] = (hat2 * s.g2[...]).astype(BF).reshape(NH, ROWS, WIDTH)
    over_y = gather_y_start(s.nf2)
    settle()
    for copy in over_y:
        copy.wait_recv()
    hidden_pre = mm(s.nf2[...].reshape(128, WIDTH), s.wu[...])
    hidden, slope = gelu_both(hidden_pre)
    s.hid[...] = hidden.astype(BF)
    grad_pre = (slope * grad_hidden).astype(BF)
    over_y = sum_tok_start(1, mm_nt(grad_pre, s.wu[...]))
    out_y = []

    def out_start():
        out_y.extend(sum_tok_start(2, mm(s.hid[...], s.wd[...])))

    grad_normed = sum_tok_both(1, over_y, out_start)
    both_cot = s.cot[y].astype(F32).reshape(2 * ROWS, WIDTH)
    grad_second = both_cot + norm_back(grad_normed, both_rows(s.xh2), rstd2, s.g2[...])
    s.gsec[...] = grad_second.reshape(NH, ROWS, WIDTH)
    s.gsa[y] = grad_second.astype(BF).reshape(NH, ROWS, WIDTH)
    over_y = gather_y_start(s.gsa)
    settle()
    out_state = sum_tok_pass(2, out_y)
    for copy in over_y:
        copy.wait_recv()

    grad_att = mm_nt(s.gsa[...].reshape(128, WIDTH), s.wo[...]).astype(BF)
    grad_over = (grad_att.astype(F32) * s.inv[...]).astype(BF)
    s.gb[...] = by_head(grad_over.astype(F32))
    product = jnp.transpose(grad_over.astype(F32) * s.att[...])
    delta = jnp.concatenate(
        [
            jnp.sum(product[0:SIZE], axis=0, keepdims=True),
            jnp.sum(product[SIZE:128], axis=0, keepdims=True),
        ],
        axis=1,
    )
    s.tot[0:1, :] = delta
    s.numt[...] = jnp.zeros((128, 256), F32)

    def value_back(xk):
        for i in range(2):
            pair = pl.ds(i * 2, 2)
            e_b = s.es[xk, pair].reshape(512, 256)
            s.dpv[pair, xk] = mm(e_b, s.gb[...]).astype(BF).reshape(2, NC, 128, 128)

    def key_back(xk):
        for i in range(2):
            pair = pl.ds(i * 2, 2)
            block = s.kvb[pair, xk].reshape(512, 256)
            e_b = s.es[xk, pair].reshape(512, 256)
            ahead = mm_nt(block[:, 128:256], s.gb[...])
            d_b = (e_b.astype(F32) * (ahead - s.tot[0:1, :])).astype(BF)
            s.dpk[pair, xk] = mm(d_b, s.qs[...]).astype(BF).reshape(2, NC, 128, 128)
            s.numt[...] += mm(jnp.transpose(block[:, 0:128].astype(F32)).astype(BF), d_b)

    v_sum = VarSum(s.dpv, s.rcv, s.s1v, s.rmv, s.rxv, s.ownv, s.s2v, s.rzv)
    k_sum = VarSum(s.dpk, s.rck, s.s1k, s.rmk, s.rxk, s.ownk, s.s2k, s.rzk)
    for k, before in ((2, None), (1, 2), (3, 1), (0, 3)):
        value_back(turn(x, k))
        v_sum.put(k)
        if before is not None:
            v_sum.finish(before)
    key_back(turn(x, 2))
    k_sum.put(2)
    v_sum.finish(0)
    v_sum.relay()
    key_back(turn(x, 1))
    k_sum.put(1)
    k_sum.finish(2)
    key_back(turn(x, 3))
    k_sum.put(3)
    k_sum.finish(1)
    key_back(x)
    k_sum.put(0)
    k_sum.finish(3)
    k_sum.relay()
    k_sum.finish(0)
    settle()
    v_sum.along_z()
    k_sum.along_z()
    own_v = v_sum.end()
    own_k = k_sum.end()
    grad_query = jnp.transpose(own_head(s.numt[...])) * SCALE
    grad_qkv = jnp.concatenate(
        [grad_query.astype(BF), own_k.astype(BF), own_v.astype(BF)], axis=1
    )
    over_y = sum_tok_start(3, mm_nt(grad_qkv, s.wq[...]))
    s.out_ref[...] = (s.xb[h] + sum_tok_end(2, out_state)).astype(BF)
    grad_normed = sum_tok_end(3, sum_tok_pass(3, over_y))
    grad_first = s.gsec[h] + norm_back(grad_normed, s.xh1[...], rstd1, s.g1[...])

    grad_picked = mm_nt(grad_first.astype(BF), s.aout[...]).astype(BF)
    inner = mm_nt((grad_picked.astype(F32) * s.picked[...]).astype(BF), s.spread[0] + s.spread[1])
    s.gpb[z, x, c] = jnp.concatenate([grad_picked, inner.astype(BF)], axis=1)
    gp_state = gather_var_start(s.gpb, True)
    rows_k = lax.broadcasted_iota(jnp.int32, (128, WIDTH), 0)
    keys8 = jnp.concatenate([s.akey[...]] * 8, axis=0)
    s.kext[...] = jnp.where(rows_k < 32, keys8.astype(F32), 0.0).astype(BF)
    gather_var_pass(gp_state)

    def pool_back(xk):
        block = s.gpb[:, xk].reshape(128, GWIDTH)
        grad = block[:, 0:WIDTH].astype(F32)
        probs = s.prl[:, xk].reshape(128, 128)
        probs_b = probs.astype(BF)
        ahead = None
        for j in range(2):
            term = (grad * s.vals[j, :, xk].reshape(128, WIDTH).astype(F32)).astype(BF)
            term = mm_nt(term, s.spread[j])
            ahead = term if ahead is None else ahead + term
            wide = mm(probs_b, s.spread[j])
            s.zs[j, :, xk] = (wide * grad).astype(BF).reshape(NZ, 32, WIDTH)
        scores = probs * (ahead - block[:, WIDTH:GWIDTH].astype(F32)) * SCALE
        s.gps[:, xk] = scores.astype(BF).reshape(NZ, 32, 128)

    gather_var_end(gp_state)
    gather_var_core(gp_state, 0)
    pool_back(x)
    gather_var_core(gp_state, 1)
    pool_back(turn(x, 3))
    gather_var_far(gp_state)
    gather_var_core(gp_state, 3)
    pool_back(turn(x, 1))
    gather_var_core(gp_state, 2)
    pool_back(turn(x, 2))

    key_part = mm(s.px[...].reshape(2 * EXT, SPAN), s.gps[...].reshape(SPAN, 128))
    rows160 = lax.broadcasted_iota(jnp.int32, (2 * EXT, 128), 0) // EXT
    lanes160 = lax.broadcasted_iota(jnp.int32, (2 * EXT, 128), 1) // 16
    key_part = jnp.where(rows160 == lanes160, key_part, 0.0).astype(BF)
    value_part = jnp.concatenate(
        [mm(s.px[j], s.zs[j].reshape(SPAN, WIDTH)).astype(BF) for j in range(2)], axis=0
    )
    for n in range(4):
        cols = pl.ds(n * 256, 256)
        term = mm_nt(value_part, s.aval[cols, :]) + mm(key_part, s.kext[:, cols])
        term = term.astype(BF)
        for i in range(2):
            s.fsrc[n, i] = term[:, i * 128 : (i + 1) * 128]
    last = [
        send(s.fsrc.at[turn(y, k)], s.fry.at[k - 1], dev(yy=turn(y, k))) for k in (2, 1, 3)
    ]
    settle()
    for copy in last:
        copy.wait_recv()

    def here(hh):
        return (
            s.fsrc[y, hh].astype(F32)
            + s.fry[0, hh].astype(F32)
            + s.fry[1, hh].astype(F32)
            + s.fry[2, hh].astype(F32)
        )

    s.fsz[...] = here(1 - h).astype(BF)
    copy = send(s.fsz, s.frz, partner)
    mine = here(h)
    settle()
    copy.wait_recv()
    final = mine + s.frz[...].astype(F32)
    s.sum_ref[...] = final
    for copy in started[settled[0] :]:
        copy.wait_send()


def finish_kernel(out_ref, sum_ref, block_ref, embed_ref, var_ref):
    block_ref[...] = out_ref[...]
    for j in range(2):
        embed_ref[j] = sum_ref[j * EXT : j * EXT + PIX]
        var_ref[j : j + 1, :] = sum_ref[j * EXT + PIX : j * EXT + PIX + 1]


def local(
    patches,
    embed_weight,
    var_embed,
    agg_keys,
    agg_value,
    agg_out,
    pos_embed,
    norm_first,
    norm_second,
    w_qkv,
    w_out,
    w_up,
    w_down,
    cotangent,
):
    anywhere = pl.BlockSpec(memory_space=pl.ANY)
    vmem = pl.BlockSpec(memory_space=pltpu.VMEM)
    results = pl.pallas_call(
        kernel,
        out_shape=(
            jax.ShapeDtypeStruct((ROWS, WIDTH), BF),
            jax.ShapeDtypeStruct((2 * EXT, 128), F32),
        ),
        in_specs=[anywhere] * 14,
        out_specs=(vmem, vmem),
        scratch_shapes=[pltpu.VMEM(shape, dtype) for shape, dtype in SCRATCH.values()]
        + [
            pltpu.SemaphoreType.DMA((LINKS,)),
            pltpu.SemaphoreType.DMA((LINKS,)),
            pltpu.SemaphoreType.DMA((20,)),
        ],
        compiler_params=pltpu.CompilerParams(
            collective_id=0, has_side_effects=True, vmem_limit_bytes=56 * 1024 * 1024
        ),
    )(
        patches,
        embed_weight.reshape(2 * PIX, WIDTH),
        var_embed,
        agg_keys,
        agg_value,
        agg_out,
        pos_embed,
        norm_first.reshape(1, WIDTH),
        norm_second.reshape(1, WIDTH),
        w_qkv,
        w_out,
        w_up,
        w_down,
        cotangent,
    )
    return pl.pallas_call(
        finish_kernel,
        out_shape=(
            jax.ShapeDtypeStruct((ROWS, WIDTH), BF),
            jax.ShapeDtypeStruct((2, PIX, 128), F32),
            jax.ShapeDtypeStruct((2, 128), F32),
        ),
        in_specs=[vmem, vmem],
        out_specs=(vmem, vmem, vmem),
    )(*results)


def solution(mesh):
    in_specs = (
        P("var", None, "tok"),
        P("var", None, None),
        P("var", None),
        P(),
        P(),
        P(),
        P(("tok", "var"), None),
        P(),
        P(),
        P(None, None, "tok"),
        P("tok", None),
        P(None, "tok"),
        P("tok", None),
        P(("tok", "var"), None),
    )
    out_specs = (P(("tok", "var"), None), P("var", None, "tok"), P("var", "tok"))
    return jax.shard_map(local, mesh=mesh, in_specs=in_specs, out_specs=out_specs, check_vma=False)
```

```python
import jax
import jax.numpy as jnp
from jax import lax
from jax.experimental import pallas as pl
from jax.experimental.pallas import tpu as pltpu
from jax.sharding import PartitionSpec as P

EPS = 1e-05
MESH = pl.DeviceIdType.MESH
BF = jnp.bfloat16
F32 = jnp.float32

NZ, NX, NC, NY, NH = 4, 4, 2, 4, 2
ROWS, WIDTH, HEADS, SIZE, PIX = 16, 1024, 16, 64, 64
SPAN = 512
EXT = 80
GWIDTH = WIDTH + 128
LINKS = 160
SCALE = SIZE ** (-0.5)


def mm(a, b):
    return lax.dot_general(a, b, (((1,), (0,)), ((), ())), preferred_element_type=F32)


def mm_nt(a, b):
    return lax.dot_general(a, b, (((1,), (1,)), ((), ())), preferred_element_type=F32)


def norm_parts(values):
    mean = jnp.mean(values, axis=-1, keepdims=True)
    centred = values - mean
    spread = jnp.mean(centred * centred, axis=-1, keepdims=True)
    rstd = lax.rsqrt(spread + EPS)
    return centred * rstd, rstd


def norm_back(grad, hat, rstd, gain):
    inner = grad * gain
    first = jnp.mean(inner, axis=-1, keepdims=True)
    second = jnp.mean(inner * hat, axis=-1, keepdims=True)
    return rstd * (inner - first - hat * second)


def gelu_both(values):
    c = 0.7978845608028654
    a = 0.044715
    square = values * values
    t = jnp.tanh(c * values * (1.0 + a * square))
    half = 0.5 * (1.0 + t)
    slope = half + 0.5 * values * (1.0 - t * t) * c * (1.0 + 3.0 * a * square)
    return values * half, slope


SCRATCH = dict(
    px=((2, EXT, SPAN), BF),
    wx=((128, WIDTH), BF),
    akey=((16, WIDTH), BF),
    vemb=((2, WIDTH), F32),
    aval=((WIDTH, WIDTH), BF),
    aout=((WIDTH, WIDTH), BF),
    posv=((ROWS, WIDTH), BF),
    g1=((1, WIDTH), F32),
    g2=((1, WIDTH), F32),
    wq=((WIDTH, 384), BF),
    wo=((128, WIDTH), BF),
    wu=((WIDTH, 512), BF),
    wd=((512, WIDTH), BF),
    tsend=((2, 16, SPAN), BF),
    trecv=((10, 16, SPAN), BF),
    town=((16, SPAN), F32),
    expo=((32, SPAN), F32),
    ub=((2, 128, WIDTH), BF),
    ubias=((16, WIDTH), F32),
    ptl=((NZ, NX, 32, 128), BF),
    prl=((NZ, NX, 32, 128), F32),
    spread=((2, 128, WIDTH), BF),
    vals=((2, NZ, NX, 32, WIDTH), BF),
    part=((NZ, NX, NC, ROWS, WIDTH), BF),
    rc1=((NX, NZ, ROWS, WIDTH), BF),
    s1=((NX - 1, NZ, ROWS, WIDTH), BF),
    rx1=((3, NZ, ROWS, WIDTH), BF),
    own1=((NZ, ROWS, WIDTH), F32),
    s2=((NZ - 1, ROWS, WIDTH), BF),
    rz1=((NZ - 1, ROWS, WIDTH), BF),
    picked=((ROWS, WIDTH), F32),
    xh1=((ROWS, WIDTH), F32),
    xh2=((NH, ROWS, WIDTH), F32),
    xa=((NH, ROWS, WIDTH), F32),
    xb=((NH, ROWS, WIDTH), F32),
    gsec=((NH, ROWS, WIDTH), F32),
    xnear=((ROWS, WIDTH), BF),
    xfar=((ROWS, WIDTH), BF),
    bsz=((2, NH, ROWS, WIDTH), BF),
    brz=((2, NH, ROWS, WIDTH), BF),
    nf1=((NY, NH, ROWS, WIDTH), BF),
    cot=((NY, NH, ROWS, WIDTH), BF),
    nf2=((NY, NH, ROWS, WIDTH), BF),
    gsa=((NY, NH, ROWS, WIDTH), BF),
    tsrc=((4, NY, NH, ROWS, WIDTH), BF),
    try_=((4, NY - 1, NH, ROWS, WIDTH), BF),
    tsz=((4, ROWS, WIDTH), BF),
    trz=((4, ROWS, WIDTH), BF),
    fsrc=((NY, NH, 2 * EXT, 128), BF),
    fry=((NY - 1, NH, 2 * EXT, 128), BF),
    fsz=((2 * EXT, 128), BF),
    frz=((2 * EXT, 128), BF),
    qs=((256, 128), BF),
    kvb=((NZ, NX, NC, 128, 256), BF),
    es=((NX, NZ, 256, 256), BF),
    numt=((128, 256), F32),
    tot=((8, 256), F32),
    inv=((128, 128), F32),
    att=((128, 128), F32),
    gb=((256, 128), BF),
    dpk=((NZ, NX, NC, 128, 128), BF),
    rck=((NX, NZ, 128, 128), BF),
    s1k=((NX - 1, NZ, 128, 128), BF),
    rmk=((2, NZ // 2, 128, 128), BF),
    rxk=((2, NZ, 128, 128), BF),
    ownk=((NZ, 128, 128), F32),
    s2k=((NZ - 1, 128, 128), BF),
    rzk=((NZ - 1, 128, 128), BF),
    dpv=((NZ, NX, NC, 128, 128), BF),
    rcv=((NX, NZ, 128, 128), BF),
    s1v=((NX - 1, NZ, 128, 128), BF),
    rmv=((2, NZ // 2, 128, 128), BF),
    rxv=((2, NZ, 128, 128), BF),
    ownv=((NZ, 128, 128), F32),
    s2v=((NZ - 1, 128, 128), BF),
    rzv=((NZ - 1, 128, 128), BF),
    hid=((128, 512), BF),
    gpb=((NZ, NX, NC, ROWS, GWIDTH), BF),
    zs=((2, NZ, NX, 32, WIDTH), BF),
    gps=((NZ, NX, 32, 128), BF),
    kext=((128, WIDTH), BF),
)


ARGS = (
    "patches",
    "embed",
    "var_e",
    "keys",
    "a_val",
    "a_out",
    "pos",
    "n1",
    "n2",
    "wqkv",
    "w_out",
    "w_up",
    "w_down",
    "cotangent",
)
OUTS = ("out_ref", "sum_ref")


class Refs:
    pass


def kernel(*refs):
    names = ARGS + OUTS + tuple(SCRATCH)
    s = Refs()
    for name, ref in zip(names, refs):
        setattr(s, name, ref)
    send_sems, recv_sems, load_sems = refs[len(names) :]

    v = lax.axis_index("var")
    t = lax.axis_index("tok")
    c = lax.rem(v, 2)
    x = lax.rem(lax.div(v, 2), 4)
    z = lax.div(v, 8)
    y = lax.div(t, 2)
    h = lax.rem(t, 2)

    def turn(i, k):
        return lax.rem(i + k, 4)

    def dev(zz=None, xx=None, cc=None, yy=None, hh=None):
        zz = z if zz is None else zz
        xx = x if xx is None else xx
        cc = c if cc is None else cc
        yy = y if yy is None else yy
        hh = h if hh is None else hh
        return ((zz * 4 + xx) * 2 + cc, yy * 2 + hh)

    sibling = dev(cc=1 - c)
    partner = dev(hh=1 - h)
    started = []

    def send(src, dst, device):
        index = len(started)
        copy = pltpu.make_async_remote_copy(
            src_ref=src,
            dst_ref=dst,
            send_sem=send_sems.at[index],
            recv_sem=recv_sems.at[index],
            device_id=device,
            device_id_type=MESH,
        )
        copy.start()
        started.append(copy)
        return copy

    settled = [0, 0]

    def settle():
        for copy in started[settled[0] : settled[1]]:
            copy.wait_send()
        settled[:] = settled[1], len(started)

    loads = []

    def load(src, dst):
        copy = pltpu.make_async_copy(src, dst, load_sems.at[len(loads)])
        copy.start()
        loads.append(copy)
        return copy

    l_first = [
        load(s.keys, s.akey),
        load(s.embed, s.wx),
        load(s.patches.at[0], s.px.at[0, pl.ds(0, PIX)]),
        load(s.patches.at[1], s.px.at[1, pl.ds(0, PIX)]),
        load(s.var_e, s.vemb),
    ]
    l_val = load(s.a_val, s.aval)
    l_cot = load(s.cotangent, s.cot.at[y, h])
    l_mix = [load(s.a_out, s.aout), load(s.pos, s.posv), load(s.n1, s.g1)]
    l_qkv = [load(s.wqkv.at[i], s.wq.at[:, pl.ds(i * 128, 128)]) for i in range(3)]
    l_wo = load(s.w_out, s.wo)
    l_mlp = [load(s.n2, s.g2), load(s.w_up, s.wu), load(s.w_down, s.wd)]

    peers = [sibling, partner]
    for k in (1, 2, 3):
        peers += [dev(zz=turn(z, k)), dev(xx=turn(x, k)), dev(yy=turn(y, k))]
        peers += [dev(xx=turn(x, k), cc=1 - c)]
    barrier = pltpu.get_barrier_semaphore()
    for peer in peers:
        pl.semaphore_signal(barrier, inc=1, device_id=peer, device_id_type=MESH)

    lane_head = lax.broadcasted_iota(jnp.int32, (128, WIDTH), 1) // SIZE
    row = lax.broadcasted_iota(jnp.int32, (128, WIDTH), 0)
    for i in range(2):
        s.spread[i] = jnp.where(row == lane_head + i * 16, 1.0, 0.0).astype(BF)
        ones = lax.broadcasted_iota(jnp.int32, (EXT - PIX, SPAN), 0)
        s.px[i, PIX:EXT] = jnp.where(ones == 0, 1.0, 0.0).astype(BF)

    for copy in l_first:
        copy.wait()
    key_t = mm_nt(s.akey[...], s.wx[...])
    both = jnp.concatenate([key_t, key_t], axis=0)
    rows32 = lax.broadcasted_iota(jnp.int32, (32, 128), 0) // 16
    lanes32 = lax.broadcasted_iota(jnp.int32, (32, 128), 1) // PIX
    both = jnp.where(rows32 == lanes32, both, 0.0).astype(BF)
    rows16 = lax.broadcasted_iota(jnp.int32, (16, WIDTH), 0)
    var_rows = jnp.where(
        rows16 == 0, s.vemb[0:1, :], jnp.where(rows16 == 1, s.vemb[1:2, :], 0.0)
    ).astype(BF)
    key_bias = mm_nt(s.akey[...], var_rows)
    bias32 = jnp.concatenate([key_bias[:, 0:1], key_bias[:, 1:2]], axis=0)
    pixels = jnp.concatenate([s.px[0, 0:PIX], s.px[1, 0:PIX]], axis=0)
    expo = jnp.exp((mm(both, pixels) + bias32) * SCALE)
    s.expo[...] = expo
    s.town[...] = expo[0:16] + expo[16:32]
    s.tsend[0] = s.town[...].astype(BF)
    s.ptl[...] = jnp.transpose(pixels).reshape(NZ, NX, 32, 128)

    pl.semaphore_wait(barrier, len(peers))
    t_near = [send(s.tsend.at[0], s.trecv.at[0], sibling)]
    for k in (2, 1, 3):
        t_near.append(send(s.tsend.at[0], s.trecv.at[2 * k - 1], dev(xx=turn(x, k))))
        t_near.append(send(s.tsend.at[0], s.trecv.at[2 * k], dev(xx=turn(x, k), cc=1 - c)))

    def gather_tok_start(buf):
        first = send(buf.at[y, h], buf.at[y, h], partner)
        direct = [
            send(buf.at[y, h], buf.at[y, h], dev(yy=turn(y, k))) for k in (2, 1, 3)
        ]
        return buf, first, direct

    def gather_tok_end(state):
        buf, first, direct = state
        first.wait_recv()
        settle()
        passed = [
            send(buf.at[y, 1 - h], buf.at[y, 1 - h], dev(yy=turn(y, k))) for k in (2, 1, 3)
        ]
        for copy in direct + passed:
            copy.wait_recv()

    l_cot.wait()
    l_val.wait()
    bias = mm(var_rows, s.aval[...])
    s.ubias[...] = bias
    row_var = lax.broadcasted_iota(jnp.int32, (128, 256), 0) // PIX
    for n in range(4):
        cols = pl.ds(n * 256, 256)
        u = mm(s.wx[...], s.aval[:, cols])
        for i in range(2):
            s.ub[i, :, cols] = jnp.where(row_var == i, u, 0.0).astype(BF)

    def value_step(i, carry):
        lhs = s.ptl[i].reshape(128, 128)
        for j in range(2):
            out = mm(lhs, s.ub[j]) + s.ubias[j : j + 1, :]
            s.vals[j, i] = out.astype(BF).reshape(NX, 32, WIDTH)
        return carry

    lax.fori_loop(0, 2, value_step, 0)
    for copy in t_near:
        copy.wait_recv()
    near = s.town[...]
    for i in range(7):
        near = near + s.trecv[i].astype(F32)
    s.town[...] = near
    s.tsend[1] = near.astype(BF)
    t_z = [send(s.tsend.at[1], s.trecv.at[6 + k], dev(zz=turn(z, k))) for k in (2, 1, 3)]
    lax.fori_loop(2, 4, value_step, 0)
    for copy in t_z:
        copy.wait_recv()
    total = s.town[...]
    for i in range(7, 10):
        total = total + s.trecv[i].astype(F32)
    probs = s.expo[...] / jnp.concatenate([total, total], axis=0)
    probs = jnp.concatenate([probs, jnp.zeros((96, SPAN), F32)], axis=0)
    s.prl[...] = jnp.transpose(probs).reshape(NZ, NX, 32, 128)

    class VarSum:
        def __init__(self, part, rc, s1, rm, rx, own, s2, rz):
            self.part, self.rc, self.s1, self.rm = part, rc, s1, rm
            self.rx, self.own, self.s2, self.rz = rx, own, s2, rz
            self.core, self.middle, self.over_x, self.over_z = {}, {}, [], []
            self.right, self.left = dev(xx=turn(x, 1)), dev(xx=turn(x, 3))
            self.low, self.high = pl.ds(0, NZ // 2), pl.ds(NZ // 2, NZ // 2)

        def put(self, k):
            self.core[k] = send(self.part.at[:, turn(x, k), 1 - c], self.rc.at[k], sibling)

        def pass_x(self, src, dst, device):
            self.over_x.append(send(src, dst, device))

        def finish(self, k):
            self.core[k].wait_recv()
            s1, rx, low, high = self.s1, self.rx, self.low, self.high
            total = self.part[:, turn(x, k), c].astype(F32) + self.rc[k].astype(F32)
            if k == 0:
                self.own[...] = total
                return
            s1[k - 1] = total.astype(BF)
            if self.rm is None:
                self.pass_x(s1.at[k - 1], rx.at[k - 1], dev(xx=turn(x, k)))
            elif k == 2:
                self.middle[1] = send(s1.at[1, low], self.rm.at[0], self.right)
                self.middle[3] = send(s1.at[1, high], self.rm.at[1], self.left)
            elif k == 1:
                self.pass_x(s1.at[0, high], rx.at[0, high], self.right)
            else:
                self.pass_x(s1.at[2, low], rx.at[1, low], self.left)

        def relay(self):
            if self.rm is None:
                return
            s1, rm, rx, low, high = self.s1, self.rm, self.rx, self.low, self.high
            self.middle[1].wait_recv()
            s1[0, low] = (s1[0, low].astype(F32) + rm[0].astype(F32)).astype(BF)
            self.pass_x(s1.at[0, low], rx.at[0, low], self.right)
            self.middle[3].wait_recv()
            s1[2, high] = (s1[2, high].astype(F32) + rm[1].astype(F32)).astype(BF)
            self.pass_x(s1.at[2, high], rx.at[1, high], self.left)

        def here(self, zk):
            total = self.own[zk]
            for i in range(self.rx.shape[0]):
                total = total + self.rx[i, zk].astype(F32)
            return total

        def along_z(self):
            for copy in self.over_x:
                copy.wait_recv()
            for k in (2, 1, 3):
                zk = turn(z, k)
                self.s2[k - 1] = self.here(zk).astype(BF)
                self.over_z.append(send(self.s2.at[k - 1], self.rz.at[k - 1], dev(zz=zk)))

        def end(self):
            mine = self.here(z)
            settle()
            for copy in self.over_z:
                copy.wait_recv()
            rz = self.rz
            return mine + rz[0].astype(F32) + rz[1].astype(F32) + rz[2].astype(F32)

    def pool_produce(xk):
        probs_b = s.prl[:, xk].reshape(128, 128).astype(BF)
        acc = None
        for j in range(2):
            term = mm(probs_b, s.spread[j]) * s.vals[j, :, xk].reshape(128, WIDTH).astype(F32)
            acc = term if acc is None else acc + term
        s.part[:, xk] = acc.astype(BF).reshape(NZ, NC, ROWS, WIDTH)

    cot_state = gather_tok_start(s.cot)
    pool_sum = VarSum(s.part, s.rc1, s.s1, None, s.rx1, s.own1, s.s2, s.rz1)
    for k, before in ((2, None), (1, 2), (3, 1), (0, 3)):
        pool_produce(turn(x, k))
        pool_sum.put(k)
        if before is not None:
            pool_sum.finish(before)
    pool_sum.finish(0)
    settle()
    pool_sum.along_z()
    picked = pool_sum.end()
    picked_b = picked.astype(BF)
    s.picked[...] = picked_b.astype(F32)

    for copy in l_mix:
        copy.wait()
    x_first = mm(picked_b, s.aout[...]) + s.posv[...].astype(F32)
    s.xa[h] = x_first
    s.xnear[...] = x_first.astype(BF)
    hat, rstd1 = norm_parts(x_first)
    s.xh1[...] = hat
    s.nf1[y, h] = (hat * s.g1[...]).astype(BF)
    state = gather_tok_start(s.nf1)
    gather_tok_end(cot_state)
    x_copy = send(s.xnear, s.xfar, partner)
    gather_tok_end(state)
    for copy in l_qkv:
        copy.wait()
    qkv = mm(s.nf1[...].reshape(128, WIDTH), s.wq[...])
    s.kvb[z, x, c] = qkv[:, 128:384].astype(BF)

    def gather_var_start(buf, direct):
        mine = buf.at[z, x, c]
        right, left = dev(xx=turn(x, 1)), dev(xx=turn(x, 3))
        over_z = [send(mine, mine, dev(zz=turn(z, k))) for k in (1, 2, 3)]
        over_x = {(0, 1): send(mine, mine, right), (0, 3): send(mine, mine, left)}
        if direct:
            over_x[0, 2] = send(mine, mine, dev(xx=turn(x, 2)))
        over_c = {(0, 0): send(mine, mine, sibling)}
        settle()
        return buf, over_z, over_x, over_c, direct

    def gather_var_pass(state):
        buf, over_z, over_x, over_c, direct = state
        right, left = dev(xx=turn(x, 1)), dev(xx=turn(x, 3))
        for kz in (1, 3, 2):
            over_z[kz - 1].wait_recv()
            block = buf.at[turn(z, 4 - kz), x, c]
            over_x[kz, 1] = send(block, block, right)
            over_x[kz, 3] = send(block, block, left)
            if direct:
                over_x[kz, 2] = send(block, block, dev(xx=turn(x, 2)))
            over_c[kz, 0] = send(block, block, sibling)

    def gather_var_end(state):
        buf, over_z, over_x, over_c, direct = state
        right, left = dev(xx=turn(x, 1)), dev(xx=turn(x, 3))
        for kz in (0, 1, 3, 2):
            for kx in (1, 3):
                over_x[kz, kx].wait_recv()
                block = buf.at[turn(z, 4 - kz), turn(x, 4 - kx), c]
                if kx == 1 and kz in (0, 1) and not direct:
                    over_x[kz, 2] = send(block, block, right)
                if kx == 3 and kz in (2, 3) and not direct:
                    over_x[kz, 2] = send(block, block, left)
                over_c[kz, kx] = send(block, block, sibling)

    def gather_var_far(state):
        buf, over_z, over_x, over_c, direct = state
        for kz in (0, 1, 3, 2):
            over_x[kz, 2].wait_recv()
            block = buf.at[turn(z, 4 - kz), turn(x, 2), c]
            over_c[kz, 2] = send(block, block, sibling)

    def gather_var_core(state, kx):
        for kz in range(4):
            state[3][kz, kx].wait_recv()

    kv_state = gather_var_start(s.kvb, True)
    lane128 = lax.broadcasted_iota(jnp.int32, (128, 128), 1)
    row128 = lax.broadcasted_iota(jnp.int32, (128, 128), 0)

    def by_head(values):
        zero = jnp.zeros_like(values)
        return jnp.concatenate(
            [jnp.where(lane128 < SIZE, values, zero), jnp.where(lane128 >= SIZE, values, zero)],
            axis=0,
        ).astype(BF)

    def own_head(values):
        return jnp.where(row128 < SIZE, values[:, 0:128], values[:, 128:256])

    query = qkv[:, 0:128].astype(BF).astype(F32) * SCALE
    s.qs[...] = by_head(query)
    s.numt[...] = jnp.zeros((128, 256), F32)
    s.tot[...] = jnp.zeros((8, 256), F32)
    gather_var_pass(kv_state)

    def attend(xk):
        def step(i):
            block = s.kvb[pl.ds(i * 2, 2), xk].reshape(512, 256)
            scores = mm_nt(block[:, 0:128], s.qs[...])
            e = jnp.exp(scores)
            e_b = e.astype(BF)
            s.es[xk, pl.ds(i * 2, 2)] = e_b.reshape(2, 256, 256)
            s.tot[...] += jnp.sum(e.reshape(64, 8, 256), axis=0)
            s.numt[...] += mm(jnp.transpose(block[:, 128:256].astype(F32)).astype(BF), e_b)

        for i in range(2):
            step(i)

    gather_var_end(kv_state)
    gather_var_core(kv_state, 0)
    attend(x)
    gather_var_core(kv_state, 1)
    attend(turn(x, 3))
    gather_var_far(kv_state)
    gather_var_core(kv_state, 3)
    attend(turn(x, 1))
    gather_var_core(kv_state, 2)
    attend(turn(x, 2))

    inverse = 1.0 / jnp.sum(s.tot[...], axis=0, keepdims=True)
    inv_t = own_head(jnp.broadcast_to(inverse, (128, 256)))
    s.inv[...] = jnp.transpose(inv_t)
    att = jnp.transpose(own_head(s.numt[...]) * inv_t)
    s.att[...] = att

    def sum_tok_start(i, values):
        s.tsrc[i] = values.astype(BF).reshape(NY, NH, ROWS, WIDTH)
        return [
            send(s.tsrc.at[i, turn(y, k)], s.try_.at[i, k - 1], dev(yy=turn(y, k)))
            for k in (2, 1, 3)
        ]

    def sum_tok_pass(i, over_y):
        for copy in over_y:
            copy.wait_recv()

        def here(hh):
            return (
                s.tsrc[i, y, hh].astype(F32)
                + s.try_[i, 0, hh].astype(F32)
                + s.try_[i, 1, hh].astype(F32)
                + s.try_[i, 2, hh].astype(F32)
            )

        s.tsz[i] = here(1 - h).astype(BF)
        copy = send(s.tsz.at[i], s.trz.at[i], partner)
        return copy, here(h)

    def sum_tok_end(i, state):
        copy, mine = state
        copy.wait_recv()
        return mine + s.trz[i].astype(F32)

    def sum_tok_both(i, over_y, beside=None):
        for copy in over_y:
            copy.wait_recv()
        mine = s.tsrc[i, y].astype(F32)
        for k in range(3):
            mine = mine + s.try_[i, k].astype(F32)
        s.bsz[i] = mine.astype(BF)
        copy = send(s.bsz.at[i], s.brz.at[i], partner)
        if beside is not None:
            beside()
        settle()
        copy.wait_recv()
        return (mine + s.brz[i].astype(F32)).reshape(2 * ROWS, WIDTH)

    def gather_y_start(buf):
        return [send(buf.at[y], buf.at[y], dev(yy=turn(y, k))) for k in (2, 1, 3)]

    def both_rows(ref):
        return ref[...].reshape(2 * ROWS, WIDTH)

    l_wo.wait()
    over_y = sum_tok_start(0, mm(att.astype(BF), s.wo[...]))
    for copy in l_mlp:
        copy.wait()
    grad_hidden = mm_nt(s.cot[...].reshape(128, WIDTH), s.wd[...])
    x_copy.wait_recv()
    s.xa[1 - h] = s.xfar[...].astype(F32)
    x_second = both_rows(s.xa) + sum_tok_both(0, over_y)
    s.xb[...] = x_second.reshape(NH, ROWS, WIDTH)
    hat2, rstd2 = norm_parts(x_second)
    s.xh2[...] = hat2.reshape(NH, ROWS, WIDTH)
    s.nf2[y] = (hat2 * s.g2[...]).astype(BF).reshape(NH, ROWS, WIDTH)
    over_y = gather_y_start(s.nf2)
    settle()
    for copy in over_y:
        copy.wait_recv()
    hidden_pre = mm(s.nf2[...].reshape(128, WIDTH), s.wu[...])
    hidden, slope = gelu_both(hidden_pre)
    s.hid[...] = hidden.astype(BF)
    grad_pre = (slope * grad_hidden).astype(BF)
    over_y = sum_tok_start(1, mm_nt(grad_pre, s.wu[...]))
    out_y = []

    def out_start():
        out_y.extend(sum_tok_start(2, mm(s.hid[...], s.wd[...])))

    grad_normed = sum_tok_both(1, over_y, out_start)
    both_cot = s.cot[y].astype(F32).reshape(2 * ROWS, WIDTH)
    grad_second = both_cot + norm_back(grad_normed, both_rows(s.xh2), rstd2, s.g2[...])
    s.gsec[...] = grad_second.reshape(NH, ROWS, WIDTH)
    s.gsa[y] = grad_second.astype(BF).reshape(NH, ROWS, WIDTH)
    over_y = gather_y_start(s.gsa)
    settle()
    out_state = sum_tok_pass(2, out_y)
    for copy in over_y:
        copy.wait_recv()

    grad_att = mm_nt(s.gsa[...].reshape(128, WIDTH), s.wo[...]).astype(BF)
    grad_over = (grad_att.astype(F32) * s.inv[...]).astype(BF)
    s.gb[...] = by_head(grad_over.astype(F32))
    product = jnp.transpose(grad_over.astype(F32) * s.att[...])
    delta = jnp.concatenate(
        [
            jnp.sum(product[0:SIZE], axis=0, keepdims=True),
            jnp.sum(product[SIZE:128], axis=0, keepdims=True),
        ],
        axis=1,
    )
    s.tot[0:1, :] = delta
    s.numt[...] = jnp.zeros((128, 256), F32)

    def value_back(xk):
        for i in range(2):
            pair = pl.ds(i * 2, 2)
            e_b = s.es[xk, pair].reshape(512, 256)
            s.dpv[pair, xk] = mm(e_b, s.gb[...]).astype(BF).reshape(2, NC, 128, 128)

    def key_back(xk):
        for i in range(2):
            pair = pl.ds(i * 2, 2)
            block = s.kvb[pair, xk].reshape(512, 256)
            e_b = s.es[xk, pair].reshape(512, 256)
            ahead = mm_nt(block[:, 128:256], s.gb[...])
            d_b = (e_b.astype(F32) * (ahead - s.tot[0:1, :])).astype(BF)
            s.dpk[pair, xk] = mm(d_b, s.qs[...]).astype(BF).reshape(2, NC, 128, 128)
            s.numt[...] += mm(jnp.transpose(block[:, 0:128].astype(F32)).astype(BF), d_b)

    v_sum = VarSum(s.dpv, s.rcv, s.s1v, s.rmv, s.rxv, s.ownv, s.s2v, s.rzv)
    k_sum = VarSum(s.dpk, s.rck, s.s1k, s.rmk, s.rxk, s.ownk, s.s2k, s.rzk)
    for k, before in ((2, None), (1, 2), (3, 1), (0, 3)):
        value_back(turn(x, k))
        v_sum.put(k)
        if before is not None:
            v_sum.finish(before)
    key_back(turn(x, 2))
    k_sum.put(2)
    v_sum.finish(0)
    v_sum.relay()
    key_back(turn(x, 1))
    k_sum.put(1)
    k_sum.finish(2)
    key_back(turn(x, 3))
    k_sum.put(3)
    k_sum.finish(1)
    key_back(x)
    k_sum.put(0)
    k_sum.finish(3)
    k_sum.relay()
    k_sum.finish(0)
    settle()
    v_sum.along_z()
    k_sum.along_z()
    own_v = v_sum.end()
    own_k = k_sum.end()
    grad_query = jnp.transpose(own_head(s.numt[...])) * SCALE
    grad_qkv = jnp.concatenate(
        [grad_query.astype(BF), own_k.astype(BF), own_v.astype(BF)], axis=1
    )
    over_y = sum_tok_start(3, mm_nt(grad_qkv, s.wq[...]))
    s.out_ref[...] = (s.xb[h] + sum_tok_end(2, out_state)).astype(BF)
    grad_normed = sum_tok_end(3, sum_tok_pass(3, over_y))
    grad_first = s.gsec[h] + norm_back(grad_normed, s.xh1[...], rstd1, s.g1[...])

    grad_picked = mm_nt(grad_first.astype(BF), s.aout[...]).astype(BF)
    inner = mm_nt((grad_picked.astype(F32) * s.picked[...]).astype(BF), s.spread[0] + s.spread[1])
    s.gpb[z, x, c] = jnp.concatenate([grad_picked, inner.astype(BF)], axis=1)
    gp_state = gather_var_start(s.gpb, True)
    rows_k = lax.broadcasted_iota(jnp.int32, (128, WIDTH), 0)
    keys8 = jnp.concatenate([s.akey[...]] * 8, axis=0)
    s.kext[...] = jnp.where(rows_k < 32, keys8.astype(F32), 0.0).astype(BF)
    gather_var_pass(gp_state)

    def pool_back(xk):
        block = s.gpb[:, xk].reshape(128, GWIDTH)
        grad = block[:, 0:WIDTH].astype(F32)
        probs = s.prl[:, xk].reshape(128, 128)
        probs_b = probs.astype(BF)
        ahead = None
        for j in range(2):
            term = (grad * s.vals[j, :, xk].reshape(128, WIDTH).astype(F32)).astype(BF)
            term = mm_nt(term, s.spread[j])
            ahead = term if ahead is None else ahead + term
            wide = mm(probs_b, s.spread[j])
            s.zs[j, :, xk] = (wide * grad).astype(BF).reshape(NZ, 32, WIDTH)
        scores = probs * (ahead - block[:, WIDTH:GWIDTH].astype(F32)) * SCALE
        s.gps[:, xk] = scores.astype(BF).reshape(NZ, 32, 128)

    gather_var_end(gp_state)
    gather_var_core(gp_state, 0)
    pool_back(x)
    gather_var_core(gp_state, 1)
    pool_back(turn(x, 3))
    gather_var_far(gp_state)
    gather_var_core(gp_state, 3)
    pool_back(turn(x, 1))
    gather_var_core(gp_state, 2)
    pool_back(turn(x, 2))

    key_part = mm(s.px[...].reshape(2 * EXT, SPAN), s.gps[...].reshape(SPAN, 128))
    rows160 = lax.broadcasted_iota(jnp.int32, (2 * EXT, 128), 0) // EXT
    lanes160 = lax.broadcasted_iota(jnp.int32, (2 * EXT, 128), 1) // 16
    key_part = jnp.where(rows160 == lanes160, key_part, 0.0).astype(BF)
    value_part = jnp.concatenate(
        [mm(s.px[j], s.zs[j].reshape(SPAN, WIDTH)).astype(BF) for j in range(2)], axis=0
    )
    for n in range(4):
        cols = pl.ds(n * 256, 256)
        term = mm_nt(value_part, s.aval[cols, :]) + mm(key_part, s.kext[:, cols])
        term = term.astype(BF)
        for i in range(2):
            s.fsrc[n, i] = term[:, i * 128 : (i + 1) * 128]
    last = [
        send(s.fsrc.at[turn(y, k)], s.fry.at[k - 1], dev(yy=turn(y, k))) for k in (2, 1, 3)
    ]
    settle()
    for copy in last:
        copy.wait_recv()

    def here(hh):
        return (
            s.fsrc[y, hh].astype(F32)
            + s.fry[0, hh].astype(F32)
            + s.fry[1, hh].astype(F32)
            + s.fry[2, hh].astype(F32)
        )

    s.fsz[...] = here(1 - h).astype(BF)
    copy = send(s.fsz, s.frz, partner)
    mine = here(h)
    settle()
    copy.wait_recv()
    final = mine + s.frz[...].astype(F32)
    s.sum_ref[...] = final
    for copy in started[settled[0] :]:
        copy.wait_send()


def finish_kernel(out_ref, sum_ref, block_ref, embed_ref, var_ref):
    block_ref[...] = out_ref[...]
    for j in range(2):
        embed_ref[j] = sum_ref[j * EXT : j * EXT + PIX]
        var_ref[j : j + 1, :] = sum_ref[j * EXT + PIX : j * EXT + PIX + 1]


def local(
    patches,
    embed_weight,
    var_embed,
    agg_keys,
    agg_value,
    agg_out,
    pos_embed,
    norm_first,
    norm_second,
    w_qkv,
    w_out,
    w_up,
    w_down,
    cotangent,
):
    anywhere = pl.BlockSpec(memory_space=pl.ANY)
    vmem = pl.BlockSpec(memory_space=pltpu.VMEM)
    results = pl.pallas_call(
        kernel,
        out_shape=(
            jax.ShapeDtypeStruct((ROWS, WIDTH), BF),
            jax.ShapeDtypeStruct((2 * EXT, 128), F32),
        ),
        in_specs=[anywhere] * 14,
        out_specs=(vmem, vmem),
        scratch_shapes=[pltpu.VMEM(shape, dtype) for shape, dtype in SCRATCH.values()]
        + [
            pltpu.SemaphoreType.DMA((LINKS,)),
            pltpu.SemaphoreType.DMA((LINKS,)),
            pltpu.SemaphoreType.DMA((20,)),
        ],
        compiler_params=pltpu.CompilerParams(
            collective_id=0, has_side_effects=True, vmem_limit_bytes=56 * 1024 * 1024
        ),
    )(
        patches,
        embed_weight.reshape(2 * PIX, WIDTH),
        var_embed,
        agg_keys,
        agg_value,
        agg_out,
        pos_embed,
        norm_first.reshape(1, WIDTH),
        norm_second.reshape(1, WIDTH),
        w_qkv,
        w_out,
        w_up,
        w_down,
        cotangent,
    )
    return pl.pallas_call(
        finish_kernel,
        out_shape=(
            jax.ShapeDtypeStruct((ROWS, WIDTH), BF),
            jax.ShapeDtypeStruct((2, PIX, 128), F32),
            jax.ShapeDtypeStruct((2, 128), F32),
        ),
        in_specs=[vmem, vmem],
        out_specs=(vmem, vmem, vmem),
    )(*results)


def solution(mesh):
    in_specs = (
        P("var", None, "tok"),
        P("var", None, None),
        P("var", None),
        P(),
        P(),
        P(),
        P(("tok", "var"), None),
        P(),
        P(),
        P(None, None, "tok"),
        P("tok", None),
        P(None, "tok"),
        P("tok", None),
        P(("tok", "var"), None),
    )
    out_specs = (P(("tok", "var"), None), P("var", None, "tok"), P("var", "tok"))
    return jax.shard_map(local, mesh=mesh, in_specs=in_specs, out_specs=out_specs, check_vma=False)
```
